128 devices in a mesh: span: 16 (over y, z), normal: 8 (over x, core).
Axes of the slice: x: 4, y: 4, z: 4, core: 2. Of those that a mesh axis runs over, the one named last changes fastest.
Arguments:
- volume_fraction: float32 [256, 128, 1024], P('span', 'normal'), may hold values from 0.5 to 1.5
- droplet_momentum: float32 [3, 256, 128, 1024], P(None, 'span', 'normal'), may hold values from -0.5 to 0.5
- air_velocity: float32 [3, 256, 128, 1024], P(None, 'span', 'normal'), may hold values from -1 to 1
- drag: float32 [256, 128, 1024], P('span', 'normal'), may hold values from 0.5 to 3
- wall_owner: int32 [256, 1024, 1], P('span'), may hold values from 0 to 127; in each aligned block of 2048 rows (0 to 2047, 2048 to 4095, ..., all dimensions but the last counted through in order) at most 32 rows name the same one
- wall_face: int32 [256, 1024], P('span'), may hold values from 0 to 1023
- film: float32 [131072], P(('span', 'normal')), may hold values from 0.1 to 1
- ice: float32 [131072], P(('span', 'normal')), may hold values from 0 to 1
- cooling: float32 [131072], P(('span', 'normal')), may hold values from 0.2 to 2
- shed: float32 [131072], P(('span', 'normal')), may hold values from 0.2 to 0.8
- share: float32 [4, 131072], P(None, ('span', 'normal')), may hold values from 0.05 to 0.25
- upstream: int32 [4, 131072], P(None, ('span', 'normal')), may hold values from -1 to 131070, as said below
Outputs:
- fraction_out: float32 [256, 128, 1024], P('span', 'normal')
- momentum_out: float32 [3, 256, 128, 1024], P(None, 'span', 'normal')
- film_out: float32 [131072], P(('span', 'normal'))
- ice_out: float32 [131072], P(('span', 'normal'))
- displacement: float32 [256, 128, 1024], P('span', 'normal')
The draws below stay inside these ranges and needn't reach their ends.
Inputs may be any that keep to these rules, and one draw needn't show every extreme that they name: In each aligned block of 2048 wall rows (rows of wall_owner taken span index first, then chord index), no owner is named by more than 32 rows; every owner is named somewhere. upstream[k, f] is -1 or a face number from f - 1024 to f - 1; upstream[0, f] = f - 1 where f >= 1.
All inputs are finite; a program needn't handle non-finite values.
Results may differ from the reference program's by a relative error of at most 0.0003.
Values sent between devices are 32-bit elements; how exact they have to be, the bound alone decides.
A program may use at most 256 MiB of HBM per device.

```python
import math
import jax
import jax.numpy as jnp
import numpy as np

NZ = 1024
F_DEV = 1024
UPSTREAM = 4
SX = 256
NY = 128
FACES = 131072
BLOCK = 2048
MOST = 32
N_SPAN = 16
N_NORMAL = 8


def draw_upstream(key, part):
    faces_all = jnp.arange(FACES, dtype=jnp.int32)
    remaining = jax.random.randint(key, (UPSTREAM - 1, FACES), 2, F_DEV + 1, dtype=jnp.int32)
    offsets = jnp.concatenate([jnp.ones((1, FACES), jnp.int32), remaining], axis=0)
    linked = faces_all[None, :] - offsets
    return jnp.where(linked < 0, -1, linked).astype(jnp.int32)


def plant(array, rng, smallest, top_value):
    longest = array.shape.index(max(array.shape))
    spots = []
    for shift in (0, 1):
        where = [jax.random.randint(jax.random.fold_in(rng, axis), (), 0, length) for axis, length in enumerate(array.shape)]
        where[longest] = (where[longest] + shift) % array.shape[longest]
        spots.append(tuple(where))
    return array.at[spots[0]].set(smallest).at[spots[1]].set(top_value)


def steps_of(own_key, extent, split, low, high):
    def one(dim, parts):
        steps = jax.random.uniform(jax.random.fold_in(jax.random.fold_in(own_key, 6), dim), (parts,), jnp.float32, low / len(split), high / len(split))
        return jnp.repeat(jnp.exp(steps), extent[dim] // parts).reshape((-1,) + (1,) * (len(extent) - dim - 1))

    level = one(*split[0])
    for cut in split[1:]:
        level = level * one(*cut)
    return level


def routed_block(rng, own, number, rows, amount, top, reach, slope):
    ranking = jax.random.permutation(rng, amount)
    crowded, usual = shares(amount, rows * top, reach, slope, True), shares(amount, rows * top, reach, slope, False)
    places = jnp.arange(amount)

    def named(tallies, offset_by):
        used = int((tallies > 0).sum())
        fixed = max(1, used // 4)
        passed = fixed + (places - fixed + offset_by * (used - fixed)) % max(1, amount - fixed)
        return jnp.zeros((amount,), jnp.int32).at[ranking[jnp.where(places < fixed, places, passed)]].set(jnp.asarray(tallies, jnp.int32))

    tallies = jnp.where(number % 4 == 0, named(crowded, number // 4), named(usual, number - number // 4 - 1))
    mixed = jax.random.permutation(jax.random.fold_in(own, 3), amount)
    donor, taker = mixed[0:amount // 2 * 2:2], mixed[1:amount // 2 * 2:2]
    room = jnp.minimum(tallies[donor] - 1, reach - tallies[taker]) // 2
    room = jnp.where((donor == ranking[0]) | (taker == ranking[0]) | (tallies[taker] == 0), 0, jnp.maximum(room, 0))
    passed = jax.random.randint(jax.random.fold_in(own, 4), (amount // 2,), 0, 1 << 20) % (room + 1)
    tallies = tallies.at[donor].add(-passed).at[taker].add(passed)
    labels = jnp.searchsorted(jnp.cumsum(tallies), jnp.arange(rows * top), side="right").astype(jnp.int32)
    grid = labels.reshape(top, rows).T
    grid = grid[jax.random.permutation(jax.random.fold_in(own, 1), rows)]
    offset_by = jax.random.randint(jax.random.fold_in(own, 2), (rows, 1), 0, top)
    return jnp.take_along_axis(grid, (jnp.arange(top)[None, :] + offset_by) % top, axis=1)


def shares(amount, total, limit, skew, full):
    loads = [(1 << 20) // math.isqrt(grade ** skew) + 1 for grade in range(1, amount + 1)]
    largest = limit if full else min(limit, max(-(-total // amount), total * loads[0] // sum(loads)))
    least = 1 if total - largest >= amount - 1 else 0
    holding, spare = [largest] + [least] * (amount - 1), total - largest - least * (amount - 1)
    while spare > 0:
        movable = [i for i in range(1, amount) if holding[i] < largest] or [i for i in range(1, amount) if holding[i] < limit]
        mass, budget = sum([loads[i] for i in movable]), spare
        for i in movable:
            more = min(limit - holding[i], max(1, budget * loads[i] // mass), spare)
            holding[i] = holding[i] + more
            spare = spare - more
    return np.array(holding)


def setup_inputs(seed: int = 0) -> dict:
    key_list = jax.random.split(jax.random.key(seed), 13)
    volume_fraction = jnp.clip(0.5 + 1.0 * jax.random.uniform(key_list[0], (SX, NY, NZ), jnp.float32) ** steps_of(key_list[0], (SX, NY, NZ), ((0, 16), (1, 8)), -0.2, 0.2), 0.5, 1.5)
    droplet_momentum = jnp.clip(jax.random.uniform(key_list[1], (3, SX, NY, NZ), jnp.float32, -0.5, 0.5) * steps_of(key_list[1], (3, SX, NY, NZ), ((1, 16), (2, 8)), -0.4, 0.0), -0.5, 0.5)
    air_velocity = jnp.clip(jax.random.uniform(key_list[2], (3, SX, NY, NZ), jnp.float32, -1.0, 1.0) * steps_of(key_list[2], (3, SX, NY, NZ), ((1, 16), (2, 8)), -0.4, 0.0), -1.0, 1.0)
    drag = jnp.clip(jnp.exp(math.log(3.0) - 1.7917595 * jax.random.uniform(key_list[3], (SX, NY, NZ), jnp.float32) ** steps_of(key_list[3], (SX, NY, NZ), ((0, 16), (1, 8)), -0.2, 0.2)), 0.5, 3.0)
    wall_owner_keys = jax.random.split(jax.random.fold_in(key_list[4], 1), SX * NZ // BLOCK)
    wall_owner_turns = jax.random.permutation(jax.random.fold_in(key_list[4], 3), SX * NZ // BLOCK)
    wall_owner = jax.vmap(lambda own, number: routed_block(jax.random.fold_in(key_list[4], 2), own, number, BLOCK, N_SPAN * N_NORMAL, 1, MOST, 2))(wall_owner_keys, wall_owner_turns).reshape((SX, NZ, 1))
    wall_face = plant(jax.random.randint(key_list[5], (SX, NZ), 0, F_DEV), jax.random.fold_in(key_list[5], 1), 0, F_DEV - 1).astype(jnp.int32)
    film = jnp.clip(0.1 + 0.9 * jax.random.uniform(key_list[6], (FACES,), jnp.float32) ** steps_of(key_list[6], (FACES,), ((0, 128),), -0.2, 0.2), 0.1, 1.0)
    ice = jnp.clip(1.0 * jax.random.uniform(key_list[7], (FACES,), jnp.float32) ** steps_of(key_list[7], (FACES,), ((0, 128),), -0.2, 0.2), 0.0, 1.0)
    cooling = jnp.clip(jnp.exp(math.log(2.0) - 2.3025851 * jax.random.uniform(key_list[8], (FACES,), jnp.float32) ** steps_of(key_list[8], (FACES,), ((0, 128),), -0.2, 0.2)), 0.2, 2.0)
    shed = jnp.clip(0.2 + 0.6 * jax.random.uniform(key_list[9], (FACES,), jnp.float32) ** steps_of(key_list[9], (FACES,), ((0, 128),), -0.2, 0.2), 0.2, 0.8)
    share = jnp.clip(jnp.exp(math.log(0.25) - 1.609438 * jax.random.uniform(key_list[10], (UPSTREAM, FACES), jnp.float32) ** steps_of(key_list[10], (UPSTREAM, FACES), ((1, 128),), -0.2, 0.2)), 0.05, 0.25)
    upstream = draw_upstream(jax.random.fold_in(key_list[12], 71), 0)
    return {"volume_fraction": volume_fraction, "droplet_momentum": droplet_momentum, "air_velocity": air_velocity, "drag": drag, "wall_owner": wall_owner, "wall_face": wall_face, "film": film, "ice": ice, "cooling": cooling, "shed": shed, "share": share, "upstream": upstream}


pseudo_step = 0.15
impact_rate = 4.0


def window(padded, first, second, third):
    span_len = padded.shape[1] - 2
    normal_len = padded.shape[2] - 2
    chord_len = padded.shape[3] - 2
    return padded[:, first:first + span_len, second:second + normal_len, third:third + chord_len]


def upwind_sweep(state_pad, velocity_pad, air_velocity, drag):
    centre = window(state_pad, 1, 1, 1)
    speed_centre = window(velocity_pad, 1, 1, 1)
    divergence = jnp.zeros_like(centre)
    for direction in range(3):
        lower_at = [1, 1, 1]
        upper_at = [1, 1, 1]
        lower_at[direction] = 0
        upper_at[direction] = 2
        lower = window(state_pad, lower_at[0], lower_at[1], lower_at[2])
        upper = window(state_pad, upper_at[0], upper_at[1], upper_at[2])
        speed_lower = window(velocity_pad, lower_at[0], lower_at[1], lower_at[2])[direction]
        speed_upper = window(velocity_pad, upper_at[0], upper_at[1], upper_at[2])[direction]
        face_lower = 0.5 * (speed_lower + speed_centre[direction])
        face_upper = 0.5 * (speed_centre[direction] + speed_upper)
        flux_lower = jnp.maximum(face_lower, 0.0) * lower + jnp.minimum(face_lower, 0.0) * centre
        flux_upper = jnp.maximum(face_upper, 0.0) * centre + jnp.minimum(face_upper, 0.0) * upper
        divergence = divergence + (flux_upper - flux_lower)
    source = drag[None] * (centre[0:1] * air_velocity - centre[1:])
    advanced = centre - pseudo_step * divergence
    return jnp.concatenate([advanced[0:1], advanced[1:] + pseudo_step * source], axis=0)


def pad_volume(field):
    wrapped = jnp.concatenate([field[:, -1:], field, field[:, :1]], axis=1)
    return jnp.pad(wrapped, ((0, 0), (0, 0), (1, 1), (1, 1)))


def reference(volume_fraction, droplet_momentum, air_velocity, drag, wall_owner, wall_face, film, ice, cooling, shed, share, upstream):
    velocity = droplet_momentum / volume_fraction[None]
    droplet_state = jnp.concatenate([volume_fraction[None], droplet_momentum], axis=0)
    velocity_pad = pad_volume(velocity)
    for sweep_index in range(2):
        droplet_state = upwind_sweep(pad_volume(droplet_state), velocity_pad, air_velocity, drag)
    wall_state = droplet_state[:, :, 0, :]
    wall_speed = velocity[:, :, 0, :]
    catch = jnp.maximum(-wall_state[2], 0.0)
    kinetic = catch * 0.5 * (wall_speed[0] * wall_speed[0] + wall_speed[1] * wall_speed[1] + wall_speed[2] * wall_speed[2])
    face_index = (wall_owner[:, :, 0] * F_DEV + wall_face).reshape(-1).astype(jnp.int32)
    face_catch = jnp.zeros((FACES,), jnp.float32).at[face_index].add(catch.reshape(-1))
    face_kinetic = jnp.zeros((FACES,), jnp.float32).at[face_index].add(kinetic.reshape(-1))
    heat = cooling / (1.0 + face_kinetic)
    valid = upstream >= 0
    safe_index = jnp.maximum(upstream, 0).astype(jnp.int32)
    film_now = film
    ice_now = ice
    for sweep_index in range(2):
        outflow = film_now * shed
        arriving = jnp.where(valid, outflow[safe_index], 0.0)
        runin = jnp.sum(share * arriving, axis=0)
        inflow = impact_rate * face_catch + film_now - outflow + runin
        frozen = heat * inflow / (heat + inflow)
        film_now = inflow - frozen
        ice_now = ice_now + frozen
    row_ice = ice_now[face_index].reshape(SX, NZ)
    height = (jnp.arange(NY).astype(jnp.float32) + 0.5) / NY
    profile = (1.0 - height) * (1.0 - height)
    displacement = row_ice[:, None, :] * profile[None, :, None]
    return droplet_state[0], droplet_state[1:], film_now, ice_now, displacement
```

```python
import functools

import jax
import jax.numpy as jnp
from jax import lax
from jax.experimental import pallas as pl
from jax.experimental.pallas import tpu as pltpu
from jax.sharding import PartitionSpec as P

F32 = jnp.float32
BF16 = jnp.bfloat16
I32 = jnp.int32
MESH = pl.DeviceIdType.MESH
pseudo_step = 0.15
impact_rate = 4.0
half_step = 0.5 * pseudo_step
NX = 16
NYB = 16
NZ = 1024
LANES = 128
CH = NZ // LANES
N_SPAN = 16
N_NORMAL = 8
OWNERS = N_SPAN * N_NORMAL
SLOTS = 32
MB = 1 << 20
NT = (((1,), (1,)), ((), ()))


def iota(shape, dim):
    return lax.broadcasted_iota(I32, shape, dim)


def sweep_layer(S, V0, V1, V2, VN, NR, AIR, DRAG, emit):
    lane = iota((NYB, LANES), 1)
    row = iota((NYB, LANES), 0)
    last_lane, first_lane = lane == LANES - 1, lane == 0
    last_row, first_row = row == NYB - 1, row == 0

    def chord(c):
        zs = pl.ds(c * LANES, LANES)
        return [S(k, 0, zs) for k in range(4)] + [V2(zs)]

    here = chord(0)
    here_rolled = [pltpu.roll(t, LANES - 1, 1) for t in here]
    before = None
    for c in range(CH):
        zs = pl.ds(c * LANES, LANES)
        if c < CH - 1:
            after = chord(c + 1)
            after_rolled = [pltpu.roll(t, LANES - 1, 1) for t in after]
        else:
            after = after_rolled = [jnp.zeros((NYB, LANES), F32)] * 5
        f, v2 = here[:4], here[4]
        up = [jnp.where(last_lane, after_rolled[i], here_rolled[i]) for i in range(5)]
        w = v2 + up[4]
        pos = w > 0
        flux = [jnp.where(pos, f[k], up[k]) * w for k in range(4)]
        rolled = [pltpu.roll(t, 1, 1) for t in flux]
        if c == 0:
            edge = jnp.minimum(v2, 0.0)
            before = [edge * f[k] for k in range(4)]
        acc = [f[k] - (flux[k] - jnp.where(first_lane, before[k], rolled[k])) for k in range(4)]
        before = rolled

        v1 = V1(zs)
        w = v1 + jnp.where(last_row, VN(1, zs), pltpu.roll(v1, NYB - 1, 0))
        pos = w > 0
        w_low = VN(0, zs) + v1[0:1]
        pos_low = w_low > 0
        for k in range(4):
            upper = jnp.where(last_row, NR(1, k, zs), pltpu.roll(f[k], NYB - 1, 0))
            flux_k = jnp.where(pos, f[k], upper) * w
            low = jnp.where(pos_low, NR(0, k, zs), f[k][0:1]) * w_low
            acc[k] = acc[k] - (flux_k - jnp.where(first_row, low, pltpu.roll(flux_k, 1, 0)))

        v0 = V0(0, zs)
        w = v0 + V0(1, zs)
        w_low = V0(-1, zs) + v0
        pos, pos_low = w > 0, w_low > 0
        for k in range(4):
            flux_k = jnp.where(pos, f[k], S(k, 1, zs)) * w
            low = jnp.where(pos_low, S(k, -1, zs), f[k]) * w_low
            acc[k] = acc[k] - (flux_k - low)

        pull = pseudo_step * DRAG(zs)
        for k in range(3):
            acc[1 + k] = acc[1 + k] + pull * (f[0] * AIR(k, zs) - f[1 + k])
        emit(c, zs, acc, v0, v1, v2)
        here, here_rolled = after, after_rolled


def prep_kernel(owner_ref, face_ref, rank_ref, rank8_ref, send_ref, hq_ref):
    n = lax.axis_index("normal")
    q_len = 256
    quarters = NZ // q_len
    tri = (iota((q_len, q_len), 0) <= iota((q_len, q_len), 1)).astype(F32).astype(BF16)
    names = iota((OWNERS, q_len), 0)
    mine = N_NORMAL * iota((N_SPAN, NZ), 0) + n
    slot = iota((SLOTS, NZ), 0)
    for h in range(2):
        pieces = []
        for b in range(4):
            offset = jnp.zeros((OWNERS, 1), F32)
            got = jnp.zeros((N_SPAN, 2 * SLOTS), F32)
            for half in range(2):
                x = h * 8 + b * 2 + half
                owner = owner_ref[x]
                for q in range(quarters):
                    hot = owner[:, q * q_len : (q + 1) * q_len] == names
                    hq_ref[q * OWNERS : (q + 1) * OWNERS, :] = hot.astype(F32).astype(BF16)
                counts = jnp.dot(hq_ref[...], tri, preferred_element_type=F32)
                ranks = []
                for q in range(quarters):
                    hot = owner[:, q * q_len : (q + 1) * q_len] == names
                    part = counts[q * OWNERS : (q + 1) * OWNERS]
                    ranks.append(
                        jnp.sum(jnp.where(hot, part + offset, 0.0), axis=0, keepdims=True) - 1.0
                    )
                    offset = offset + part[:, q_len - 1 : q_len]
                rank = jnp.concatenate(ranks, axis=1).astype(I32)
                rank_ref[x] = rank
                for t in range(CH):
                    rank8_ref[x, t : t + 1, :] = rank[:, t * LANES : (t + 1) * LANES]
                face = face_ref[x : x + 1, :]
                at = slot == rank
                high = jnp.where(at, (face >> 7).astype(F32), 0.0)
                low = jnp.where(at, (face & 127).astype(F32), 0.0)
                placed = jnp.concatenate([high, low], axis=0).astype(BF16)
                hot16 = (owner == mine).astype(F32).astype(BF16)
                got = got + lax.dot_general(hot16, placed, NT, preferred_element_type=F32)
            pieces.append(got[:, :SLOTS] * 128.0 + got[:, SLOTS:])
        send_ref[:, h, :] = jnp.concatenate(pieces, axis=1).astype(I32)


def first_kernel(
    a_ref, m_ref, air_hbm, drag_hbm,
    s1_ref, v0_ref, vn_ref, nr2_ref,
    s_ref, v1_ref, v2_ref, ns_ref, nr_ref, air_ref, drag_ref,
    load_sem, air_sem, drag_sem, span_send, span_recv, normal_send, normal_recv,
):
    c, n = lax.axis_index("span"), lax.axis_index("normal")
    right, left = (c + 1) % N_SPAN, (c + N_SPAN - 1) % N_SPAN
    has_low, has_high = n > 0, n < N_NORMAL - 1

    load_a = pltpu.make_async_copy(a_ref, s_ref.at[0, pl.ds(1, NX)], load_sem.at[0])
    load_m = pltpu.make_async_copy(m_ref, s_ref.at[pl.ds(1, 3), pl.ds(1, NX)], load_sem.at[1])
    load_air = pltpu.make_async_copy(air_hbm, air_ref, air_sem)
    load_drag = pltpu.make_async_copy(drag_hbm, drag_ref, drag_sem)
    load_a.start()
    load_m.start()
    load_air.start()
    load_drag.start()

    barrier = pltpu.get_barrier_semaphore()
    for span in (left, right):
        pl.semaphore_signal(barrier, inc=1, device_id=(span, n), device_id_type=MESH)

    @pl.when(has_low)
    def _():
        pl.semaphore_signal(barrier, inc=1, device_id=(c, n - 1), device_id_type=MESH)

    @pl.when(has_high)
    def _():
        pl.semaphore_signal(barrier, inc=1, device_id=(c, n + 1), device_id_type=MESH)

    @pl.when(jnp.logical_and(has_low, has_high))
    def _():
        pl.semaphore_wait(barrier, 4)

    @pl.when(jnp.logical_not(jnp.logical_and(has_low, has_high)))
    def _():
        pl.semaphore_wait(barrier, 3)

    def span_copies(srcs, dst, base):
        copies = []
        for i, (there, layer, target) in enumerate(((right, NX, 0), (left, 1, NX + 1))):
            for j, (src, dims) in enumerate(srcs):
                copies.append(
                    pltpu.make_async_remote_copy(
                        src_ref=src(layer),
                        dst_ref=dst.at[dims, target],
                        send_sem=span_send.at[base + 2 * i + j],
                        recv_sem=span_recv.at[base + 2 * i + j],
                        device_id=(there, n),
                        device_id_type=MESH,
                    )
                )
        return copies

    def normal_copies(dst, base):
        low = pltpu.make_async_remote_copy(
            src_ref=ns_ref.at[base, 0], dst_ref=dst.at[1],
            send_sem=normal_send.at[2 * base], recv_sem=normal_recv.at[2 * base],
            device_id=(c, n - 1), device_id_type=MESH,
        )
        high = pltpu.make_async_remote_copy(
            src_ref=ns_ref.at[base, 1], dst_ref=dst.at[0],
            send_sem=normal_send.at[2 * base + 1], recv_sem=normal_recv.at[2 * base + 1],
            device_id=(c, n + 1), device_id_type=MESH,
        )
        return low, high

    def start_normal(dst, base):
        low, high = normal_copies(dst, base)

        @pl.when(has_low)
        def _():
            low.start()

        @pl.when(has_high)
        def _():
            high.start()

    def wait_normal(dst, base):
        low, high = normal_copies(dst, base)

        @pl.when(has_low)
        def _():
            low.wait_send()
            high.wait_recv()

        @pl.when(has_high)
        def _():
            high.wait_send()
            low.wait_recv()

        @pl.when(jnp.logical_not(has_low))
        def _():
            dst[0] = jnp.zeros(dst.shape[1:], F32)

        @pl.when(jnp.logical_not(has_high))
        def _():
            dst[1] = jnp.zeros(dst.shape[1:], F32)

    spans = span_copies(
        [(lambda l: a_ref.at[l - 1], 0), (lambda l: m_ref.at[:, l - 1], pl.ds(1, 3))], s_ref, 0
    )
    for copy in spans:
        copy.start()

    load_a.wait()
    load_m.wait()

    @pl.loop(0, NX)
    def _(x):
        for k in range(4):
            ns_ref[0, 0, k, x] = s_ref[k, x + 1, 0:1, :]
            ns_ref[0, 1, k, x] = s_ref[k, x + 1, NYB - 1 : NYB, :]

    start_normal(nr_ref, 0)

    @pl.loop(0, NX)
    def _(x):
        scale = half_step / s_ref[0, x + 1]
        v0_ref[x + 1] = s_ref[1, x + 1] * scale
        v1_ref[x] = s_ref[2, x + 1] * scale
        v2_ref[x] = s_ref[3, x + 1] * scale

    load_air.wait()
    load_drag.wait()
    wait_normal(nr_ref, 0)

    def edge_speed(side, present):
        @pl.when(present)
        def _():
            @pl.loop(0, NX)
            def _(x):
                vn_ref[side, x] = nr_ref[side, 2, x] * (half_step / nr_ref[side, 0, x])

        @pl.when(jnp.logical_not(present))
        def _():
            vn_ref[side] = jnp.zeros(vn_ref.shape[1:], F32)

    edge_speed(0, has_low)
    edge_speed(1, has_high)

    def layer(x):
        def emit(i, zs, acc, v0, v1, v2):
            for k in range(4):
                s1_ref[k, x, :, zs] = acc[k]
                ns_ref[1, 0, k, x - 1, :, zs] = acc[k][0:1]
                ns_ref[1, 1, k, x - 1, :, zs] = acc[k][NYB - 1 : NYB]

        sweep_layer(
            lambda k, d, zs: s_ref[k, x + d, :, zs],
            lambda d, zs: v0_ref[x + d, :, zs],
            lambda zs: v1_ref[x - 1, :, zs],
            lambda zs: v2_ref[x - 1, :, zs],
            lambda side, zs: vn_ref[side, x - 1, :, zs],
            lambda side, k, zs: nr_ref[side, k, x - 1, :, zs],
            lambda k, zs: air_ref[k, x - 1, :, zs],
            lambda zs: drag_ref[x - 1, :, zs],
            emit,
        )

    @pl.loop(0, NX)
    def _(i):
        @pl.when(i == NX - 2)
        def _():
            for copy in spans:
                copy.wait()
            for edge in (0, NX + 1):
                v0_ref[edge] = s_ref[1, edge] * (half_step / s_ref[0, edge])

        layer(jnp.where(i < NX - 2, i + 2, jnp.where(i == NX - 2, 1, NX)))

    start_normal(nr2_ref, 1)
    again = span_copies([(lambda l: s1_ref.at[:, l], pl.ds(0, 4))], s1_ref, 4)
    for copy in again:
        copy.start()
    wait_normal(nr2_ref, 1)
    for copy in again:
        copy.wait()


def second_kernel(
    sl_ref, sc_ref, su_ref, vl_ref, vc_ref, vu_ref, vn_ref, nr_ref, a_ref, m_ref, air_ref, drag_ref,
    a_out, m_out, wall_out, v1_ref, v2_ref,
):
    scale = half_step / a_ref[0]
    v1_ref[...] = m_ref[1, 0] * scale
    v2_ref[...] = m_ref[2, 0] * scale
    states = {-1: sl_ref, 0: sc_ref, 1: su_ref}
    speeds = {-1: vl_ref, 0: vc_ref, 1: vu_ref}

    def emit(i, zs, acc, v0, v1, v2):
        a_out[0, :, zs] = acc[0]
        for k in range(3):
            m_out[k, 0, :, zs] = acc[1 + k]
        catch = jnp.maximum(-acc[2][0:1], 0.0)
        s0, s1, s2 = v0[0:1], v1[0:1], v2[0:1]
        wall_out[0, 0, :, zs] = catch
        wall_out[1, 0, :, zs] = (
            catch * (0.5 / (half_step * half_step)) * (s0 * s0 + s1 * s1 + s2 * s2)
        )

    sweep_layer(
        lambda k, d, zs: states[d][k, 0, :, zs],
        lambda d, zs: speeds[d][0, :, zs],
        lambda zs: v1_ref[:, zs],
        lambda zs: v2_ref[:, zs],
        lambda side, zs: vn_ref[side, 0, :, zs],
        lambda side, k, zs: nr_ref[side, k, 0, :, zs],
        lambda k, zs: air_ref[k, 0, :, zs],
        lambda zs: drag_ref[0, :, zs],
        emit,
    )


def wall_kernel(
    wall_ref, owner_ref, owner8_ref, rank_ref, rank8_ref, sendface_ref,
    film_ref, ice_ref, cool_ref, shed_ref, share_ref, up_ref,
    film_out, ice_out, row_out,
    slots_ref, fw_ref, part_ref, got_ref, gotface_ref, lhs_ref, hot_ref, table_ref,
    links_ref, prev_ref, out_ref, back_ref, col_ref, all_ref, pick_ref,
    own_sem, sends, recvs,
):
    c, n = lax.axis_index("span"), lax.axis_index("normal")
    first_of_column, last_of_column = n == 0, n == N_NORMAL - 1
    has_next = jnp.logical_or(n < N_NORMAL - 1, c < N_SPAN - 1)
    has_prev = jnp.logical_or(n > 0, c > 0)
    next_c, next_n = jnp.where(last_of_column, c + 1, c), jnp.where(last_of_column, 0, n + 1)
    prev_c = jnp.where(first_of_column, c - 1, c)
    prev_n = jnp.where(first_of_column, N_NORMAL - 1, n - 1)
    cross_next = jnp.logical_and(last_of_column, c < N_SPAN - 1)
    cross_prev = jnp.logical_and(first_of_column, c > 0)

    barrier = pltpu.get_barrier_semaphore()

    @pl.loop(1, N_SPAN)
    def _(i):
        pl.semaphore_signal(barrier, 1, device_id=((c + i) % N_SPAN, n), device_id_type=MESH)

    @pl.loop(1, N_NORMAL)
    def _(i):
        pl.semaphore_signal(barrier, 1, device_id=(c, (n + i) % N_NORMAL), device_id_type=MESH)

    @pl.when(cross_next)
    def _():
        pl.semaphore_signal(barrier, 1, device_id=(next_c, next_n), device_id_type=MESH)

    @pl.when(cross_prev)
    def _():
        pl.semaphore_signal(barrier, 1, device_id=(prev_c, prev_n), device_id_type=MESH)

    crossing = jnp.logical_or(cross_next, cross_prev)
    peers = N_SPAN + N_NORMAL - 2

    @pl.when(crossing)
    def _():
        pl.semaphore_wait(barrier, peers + 1)

    @pl.when(jnp.logical_not(crossing))
    def _():
        pl.semaphore_wait(barrier, peers)

    def remote(src, dst, which, device):
        return pltpu.make_async_remote_copy(
            src_ref=src, dst_ref=dst, send_sem=sends.at[which], recv_sem=recvs.at[which],
            device_id=device, device_id_type=MESH,
        )

    def await_bytes(ref, sem):
        pltpu.make_async_copy(ref, ref, sem).wait()

    def to_row(src, dst, which):
        @pl.loop(1, N_SPAN)
        def _(i):
            there = (c + i) % N_SPAN
            remote(src.at[there], dst.at[c], which, (there, n)).start()

    to_row(sendface_ref, gotface_ref, 0)
    gotface_ref[c] = sendface_ref[c]

    film0 = film_ref[...]
    shed = shed_ref[...]
    out_ref[0] = film0 * shed

    @pl.when(jnp.logical_not(has_prev))
    def _():
        prev_ref[...] = jnp.zeros((2, 8, LANES), F32)

    def pass_on(step):
        return remote(out_ref.at[step], prev_ref.at[step], 1 + step, (next_c, next_n))

    @pl.when(has_next)
    def _():
        pass_on(0).start()

    for k in range(4):
        for t in range(8):
            links_ref[k, t : t + 1, :] = up_ref[k : k + 1, t * LANES : (t + 1) * LANES]
            table_ref[k, t : t + 1, :] = share_ref[k : k + 1, t * LANES : (t + 1) * LANES]

    @pl.when(first_of_column)
    def _():
        names = iota((OWNERS, NZ), 0)
        slot = iota((SLOTS, NZ), 0)

        @pl.loop(0, NX // 2)
        def _(b):
            total = jnp.zeros((4 * SLOTS, OWNERS), F32)
            for half in range(2):
                x = b * 2 + half
                owner = owner_ref[x]
                order = (owner & (N_NORMAL - 1)) * N_SPAN + (owner >> 3)
                hot = (order == names).astype(F32).astype(BF16)
                at = slot == rank_ref[x]
                rows = []
                for split in range(2):
                    for v in range(2):
                        value = wall_ref[v, x]
                        high = value.astype(BF16).astype(F32)
                        rows.append(jnp.where(at, high if split == 0 else value - high, 0.0))
                weights = jnp.concatenate(rows, axis=0).astype(BF16)
                total = total + lax.dot_general(weights, hot, NT, preferred_element_type=F32)
            both = total[: 2 * SLOTS] + total[2 * SLOTS :]
            spot = pl.ds(pl.multiple_of(b * SLOTS, SLOTS), SLOTS)
            slots_ref[0, spot, :] = both[:SLOTS]
            slots_ref[1, spot, :] = both[SLOTS:]

        for v in range(2):
            for h in range(2):
                fw_ref[:, 2 * v + h, :] = slots_ref[v, h * LANES : (h + 1) * LANES, :].T

        @pl.loop(1, N_NORMAL)
        def _(i):
            remote(fw_ref.at[pl.ds(i * N_SPAN, N_SPAN)], part_ref, 3, (c, i)).start()

        part_ref[...] = fw_ref[0:N_SPAN]

    await_bytes(gotface_ref.at[pl.ds(0, N_SPAN - 1)], recvs.at[0])
    lanes_high = iota((LANES, LANES), 0)
    for s in range(2 * N_SPAN):
        face = gotface_ref[s // 2][s % 2 : s % 2 + 1]
        hot_ref[:, s * LANES : (s + 1) * LANES] = (
            (lanes_high == (face & 127)).astype(F32).astype(BF16)
        )
        back_ref[s : s + 1, :] = face

    @pl.when(has_prev)
    def _():
        await_bytes(prev_ref.at[0], recvs.at[1])

    first_face = (c * N_NORMAL + n) * 1024

    def runin(before, own):
        total = jnp.zeros((8, LANES), F32)
        for k in range(4):
            link = links_ref[k]
            spot = link - (first_face - 1024)
            low, high = spot & 127, spot >> 7
            picked = jnp.zeros((8, LANES), F32)
            for j in range(16):
                line = before[j : j + 1] if j < 8 else own[j - 8 : j - 7]
                value = jnp.take_along_axis(
                    jnp.broadcast_to(line, (8, LANES)), low, axis=1, mode="promise_in_bounds"
                )
                picked = jnp.where(high == j, value, picked)
            total = total + table_ref[k] * jnp.where(link >= 0, picked, 0.0)
        return total

    run0 = runin(prev_ref[0], out_ref[0])

    @pl.when(jnp.logical_not(first_of_column))
    def _():
        await_bytes(part_ref, recvs.at[3])

    to_row(part_ref, got_ref, 4)
    got_ref[c] = part_ref[c]
    await_bytes(got_ref.at[pl.ds(0, N_SPAN - 1)], recvs.at[4])

    eight = iota((8, LANES), 0)
    for s in range(2 * N_SPAN):
        face_high = back_ref[s : s + 1, :] >> 7
        at = eight == face_high
        rows = []
        values = [got_ref[s // 2][2 * v + s % 2 : 2 * v + s % 2 + 1] for v in range(2)]
        highs = [value.astype(BF16).astype(F32) for value in values]
        for part in (highs, [values[v] - highs[v] for v in range(2)]):
            rows.extend(jnp.where(at, part[v], 0.0) for v in range(2))
        lhs_ref[:, s * LANES : (s + 1) * LANES] = jnp.concatenate(rows, axis=0).astype(BF16)
    sums = lax.dot_general(lhs_ref[...], hot_ref[...], NT, preferred_element_type=F32)
    sums = sums[:16] + sums[16:]
    face_catch = sums[:8]
    heat = cool_ref[...] / (1.0 + sums[8:])

    def film_step(film, outflow, run):
        inflow = impact_rate * face_catch + film - outflow + run
        frozen = heat * inflow / (heat + inflow)
        return inflow - frozen, frozen

    film1, frozen1 = film_step(film0, out_ref[0], run0)
    out_ref[1] = film1 * shed

    @pl.when(has_next)
    def _():
        pass_on(1).start()

    @pl.when(has_prev)
    def _():
        await_bytes(prev_ref.at[1], recvs.at[2])

    run1 = runin(prev_ref[1], out_ref[1])
    film2, frozen2 = film_step(film1, out_ref[1], run1)
    film_out[...] = film2
    ice2 = ice_ref[...] + frozen1 + frozen2
    ice_out[...] = ice2

    for g in range(4):
        faces = back_ref[g * 8 : g * 8 + 8, :]
        low, high = faces & 127, faces >> 7
        picked = jnp.zeros((8, LANES), F32)
        for j in range(8):
            value = jnp.take_along_axis(
                jnp.broadcast_to(ice2[j : j + 1], (8, LANES)), low, axis=1,
                mode="promise_in_bounds",
            )
            picked = jnp.where(high == j, value, picked)
        for i in range(4):
            col_ref[0, g * 4 + i] = picked[2 * i : 2 * i + 2]

    to_row(col_ref.at[0], col_ref.at[1], 5)
    col_ref[1, c] = col_ref[0, c]
    await_bytes(col_ref.at[1, pl.ds(0, N_SPAN - 1)], recvs.at[5])

    @pl.loop(1, N_NORMAL)
    def _(i):
        there = (n + i) % N_NORMAL
        remote(col_ref.at[1], all_ref.at[n], 6, (c, there)).start()

    all_ref[n] = col_ref[1]
    await_bytes(all_ref.at[pl.ds(0, N_NORMAL - 1)], recvs.at[6])

    for h in range(2):
        pick_ref[h * LANES : (h + 1) * LANES, :] = (
            all_ref[:, :, h, :].reshape(OWNERS, LANES).T
        )

    @pl.loop(0, NX)
    def _(x):
        owner = owner8_ref[x]
        order = (owner & (N_NORMAL - 1)) * N_SPAN + (owner >> 3)
        rank = rank8_ref[x]
        base = pl.multiple_of((x // 2) * SLOTS, SLOTS)
        table = pick_ref[pl.ds(base, SLOTS), :]
        picked = jnp.zeros((8, LANES), F32)
        for j in range(SLOTS):
            value = jnp.take_along_axis(
                jnp.broadcast_to(table[j : j + 1], (8, LANES)), order, axis=1,
                mode="promise_in_bounds",
            )
            picked = jnp.where(rank == j, value, picked)
        row_out[x] = picked

    await_bytes(sendface_ref.at[pl.ds(0, N_SPAN - 1)], sends.at[0])

    @pl.when(has_next)
    def _():
        await_bytes(out_ref.at[0], sends.at[1])
        await_bytes(out_ref.at[1], sends.at[2])

    @pl.when(first_of_column)
    def _():
        await_bytes(fw_ref.at[pl.ds(0, OWNERS - N_SPAN)], sends.at[3])

    await_bytes(part_ref.at[pl.ds(0, N_SPAN - 1)], sends.at[4])
    await_bytes(col_ref.at[0, pl.ds(0, N_SPAN - 1)], sends.at[5])
    await_bytes(all_ref.at[pl.ds(0, N_NORMAL - 1)], sends.at[6])


def displace_kernel(row_ref, out_ref):
    n = lax.axis_index("normal")
    y = (n * NYB + iota((NYB, LANES), 0)).astype(F32) + 0.5
    left = 1.0 - y / (NYB * N_NORMAL)
    profile = left * left
    for x in range(out_ref.shape[0]):
        for t in range(CH):
            out_ref[x, :, t * LANES : (t + 1) * LANES] = row_ref[x, t : t + 1, :] * profile


def shape(dims, dtype=F32):
    return jax.ShapeDtypeStruct(dims, dtype)


VM = pl.BlockSpec(memory_space=pltpu.VMEM)
ANY = pl.BlockSpec(memory_space=pl.ANY)


def per_device(
    volume_fraction, droplet_momentum, air_velocity, drag, wall_owner, wall_face,
    film, ice, cooling, shed, share, upstream,
):
    owner_rows = wall_owner.reshape(NX, 1, NZ)
    owner_tiles = wall_owner.reshape(NX, 8, LANES)

    rank_rows, rank_tiles, send_faces = pl.pallas_call(
        prep_kernel,
        out_shape=(
            shape((NX, 1, NZ), I32), shape((NX, 8, LANES), I32), shape((N_SPAN, 2, LANES), I32),
        ),
        in_specs=[VM] * 2,
        out_specs=(VM,) * 3,
        scratch_shapes=[pltpu.VMEM((4 * OWNERS, 256), BF16)],
        compiler_params=pltpu.CompilerParams(vmem_limit_bytes=32 * MB),
        name="slot_ranks",
    )(owner_rows, wall_face)

    brick = (NX, NYB, NZ)
    s1, v0, vn, nr2 = pl.pallas_call(
        first_kernel,
        out_shape=(
            shape((4, NX + 2, NYB, NZ)), shape((NX + 2, NYB, NZ)),
            shape((2, NX, 1, NZ)), shape((2, 4, NX, 1, NZ)),
        ),
        in_specs=[ANY] * 4,
        out_specs=(VM,) * 4,
        scratch_shapes=[
            pltpu.VMEM((4, NX + 2, NYB, NZ), F32),
            pltpu.VMEM(brick, F32),
            pltpu.VMEM(brick, F32),
            pltpu.VMEM((2, 2, 4, NX, 1, NZ), F32),
            pltpu.VMEM((2, 4, NX, 1, NZ), F32),
            pltpu.VMEM((3,) + brick, F32),
            pltpu.VMEM(brick, F32),
            pltpu.SemaphoreType.DMA((2,)),
            pltpu.SemaphoreType.DMA,
            pltpu.SemaphoreType.DMA,
            pltpu.SemaphoreType.DMA((8,)),
            pltpu.SemaphoreType.DMA((8,)),
            pltpu.SemaphoreType.DMA((4,)),
            pltpu.SemaphoreType.DMA((4,)),
        ],
        compiler_params=pltpu.CompilerParams(
            collective_id=0, has_side_effects=True, vmem_limit_bytes=48 * MB
        ),
        name="halo_sweep",
    )(volume_fraction, droplet_momentum, air_velocity, drag)

    def layers(shift):
        return pl.BlockSpec((4, 1, NYB, NZ), lambda x: (0, x + shift, 0, 0))

    def speeds(shift):
        return pl.BlockSpec((1, NYB, NZ), lambda x: (x + shift, 0, 0))

    fraction_out, momentum_out, wall = pl.pallas_call(
        second_kernel,
        out_shape=(shape(brick), shape((3,) + brick), shape((2, NX, 1, NZ))),
        grid=(NX,),
        in_specs=[layers(0), layers(1), layers(2), speeds(0), speeds(1), speeds(2),
                  pl.BlockSpec((2, 1, 1, NZ), lambda x: (0, x, 0, 0)),
                  pl.BlockSpec((2, 4, 1, 1, NZ), lambda x: (0, 0, x, 0, 0)),
                  speeds(0),
                  pl.BlockSpec((3, 1, NYB, NZ), lambda x: (0, x, 0, 0)),
                  pl.BlockSpec((3, 1, NYB, NZ), lambda x: (0, x, 0, 0)),
                  speeds(0)],
        out_specs=(speeds(0), pl.BlockSpec((3, 1, NYB, NZ), lambda x: (0, x, 0, 0)),
                   pl.BlockSpec((2, 1, 1, NZ), lambda x: (0, x, 0, 0))),
        scratch_shapes=[pltpu.VMEM((NYB, NZ), F32), pltpu.VMEM((NYB, NZ), F32)],
        compiler_params=pltpu.CompilerParams(vmem_limit_bytes=48 * MB),
        name="second_sweep",
    )(s1, s1, s1, v0, v0, v0, vn, nr2, volume_fraction, droplet_momentum, air_velocity, drag)

    tile = (8, LANES)
    film_now, ice_now, row_ice = pl.pallas_call(
        wall_kernel,
        out_shape=(shape(tile), shape(tile), shape((NX, 8, LANES))),
        in_specs=[VM] * 12,
        out_specs=(VM,) * 3,
        scratch_shapes=[
            pltpu.VMEM((2, 8 * SLOTS, OWNERS), F32),
            pltpu.VMEM((OWNERS, 4, LANES), F32),
            pltpu.VMEM((N_SPAN, 4, LANES), F32),
            pltpu.VMEM((N_SPAN, 4, LANES), F32),
            pltpu.VMEM((N_SPAN, 2, LANES), I32),
            pltpu.VMEM((32, 2 * N_SPAN * LANES), BF16),
            pltpu.VMEM((LANES, 2 * N_SPAN * LANES), BF16),
            pltpu.VMEM((4, 8, LANES), F32),
            pltpu.VMEM((4, 8, LANES), I32),
            pltpu.VMEM((2, 8, LANES), F32),
            pltpu.VMEM((2, 8, LANES), F32),
            pltpu.VMEM((2 * N_SPAN, LANES), I32),
            pltpu.VMEM((2, N_SPAN, 2, LANES), F32),
            pltpu.VMEM((N_NORMAL, N_SPAN, 2, LANES), F32),
            pltpu.VMEM((8 * SLOTS, OWNERS), F32),
            pltpu.SemaphoreType.DMA,
            pltpu.SemaphoreType.DMA((7,)),
            pltpu.SemaphoreType.DMA((7,)),
        ],
        compiler_params=pltpu.CompilerParams(
            collective_id=1, has_side_effects=True, vmem_limit_bytes=48 * MB
        ),
        name="wall_film",
    )(
        wall, owner_rows, owner_tiles, rank_rows, rank_tiles, send_faces,
        film.reshape(tile), ice.reshape(tile), cooling.reshape(tile), shed.reshape(tile),
        share, upstream,
    )

    displacement = pl.pallas_call(
        displace_kernel,
        out_shape=shape(brick),
        grid=(4,),
        in_specs=[pl.BlockSpec((NX // 4, 8, LANES), lambda i: (i, 0, 0))],
        out_specs=pl.BlockSpec((NX // 4, NYB, NZ), lambda i: (i, 0, 0)),
        name="displace",
    )(row_ice)
    return fraction_out, momentum_out, film_now.reshape(-1), ice_now.reshape(-1), displacement


def solution(mesh):
    volume = P("span", "normal", None)
    vector = P(None, "span", "normal", None)
    faces = P(("span", "normal"))
    links = P(None, ("span", "normal"))
    return jax.shard_map(
        per_device,
        mesh=mesh,
        in_specs=(
            volume, vector, vector, volume, P("span", None, None), P("span", None),
            faces, faces, faces, faces, links, links,
        ),
        out_specs=(volume, vector, faces, faces, volume),
        check_vma=False,
    )
```

```python
import functools

import jax
import jax.numpy as jnp
from jax import lax
from jax.experimental import pallas as pl
from jax.experimental.pallas import tpu as pltpu
from jax.sharding import PartitionSpec as P

F32 = jnp.float32
BF16 = jnp.bfloat16
I32 = jnp.int32
MESH = pl.DeviceIdType.MESH
pseudo_step = 0.15
impact_rate = 4.0
half_step = 0.5 * pseudo_step
NX = 16
NYB = 16
NZ = 1024
LANES = 128
CH = NZ // LANES
N_SPAN = 16
N_NORMAL = 8
OWNERS = N_SPAN * N_NORMAL
SLOTS = 32
MB = 1 << 20
NT = (((1,), (1,)), ((), ()))


def iota(shape, dim):
    return lax.broadcasted_iota(I32, shape, dim)


def sweep_layer(S, V0, V1, V2, VN, NR, AIR, DRAG, emit):
    lane = iota((NYB, LANES), 1)
    row = iota((NYB, LANES), 0)
    last_lane, first_lane = lane == LANES - 1, lane == 0
    last_row, first_row = row == NYB - 1, row == 0

    def chord(c):
        zs = pl.ds(c * LANES, LANES)
        return [S(k, 0, zs) for k in range(4)] + [V2(zs)]

    here = chord(0)
    here_rolled = [pltpu.roll(t, LANES - 1, 1) for t in here]
    before = None
    for c in range(CH):
        zs = pl.ds(c * LANES, LANES)
        if c < CH - 1:
            after = chord(c + 1)
            after_rolled = [pltpu.roll(t, LANES - 1, 1) for t in after]
        else:
            after = after_rolled = [jnp.zeros((NYB, LANES), F32)] * 5
        f, v2 = here[:4], here[4]
        up = [jnp.where(last_lane, after_rolled[i], here_rolled[i]) for i in range(5)]
        w = v2 + up[4]
        pos = w > 0
        flux = [jnp.where(pos, f[k], up[k]) * w for k in range(4)]
        rolled = [pltpu.roll(t, 1, 1) for t in flux]
        if c == 0:
            edge = jnp.minimum(v2, 0.0)
            before = [edge * f[k] for k in range(4)]
        acc = [f[k] - (flux[k] - jnp.where(first_lane, before[k], rolled[k])) for k in range(4)]
        before = rolled

        v1 = V1(zs)
        w = v1 + jnp.where(last_row, VN(1, zs), pltpu.roll(v1, NYB - 1, 0))
        pos = w > 0
        w_low = VN(0, zs) + v1[0:1]
        pos_low = w_low > 0
        for k in range(4):
            upper = jnp.where(last_row, NR(1, k, zs), pltpu.roll(f[k], NYB - 1, 0))
            flux_k = jnp.where(pos, f[k], upper) * w
            low = jnp.where(pos_low, NR(0, k, zs), f[k][0:1]) * w_low
            acc[k] = acc[k] - (flux_k - jnp.where(first_row, low, pltpu.roll(flux_k, 1, 0)))

        v0 = V0(0, zs)
        w = v0 + V0(1, zs)
        w_low = V0(-1, zs) + v0
        pos, pos_low = w > 0, w_low > 0
        for k in range(4):
            flux_k = jnp.where(pos, f[k], S(k, 1, zs)) * w
            low = jnp.where(pos_low, S(k, -1, zs), f[k]) * w_low
            acc[k] = acc[k] - (flux_k - low)

        pull = pseudo_step * DRAG(zs)
        for k in range(3):
            acc[1 + k] = acc[1 + k] + pull * (f[0] * AIR(k, zs) - f[1 + k])
        emit(c, zs, acc, v0, v1, v2)
        here, here_rolled = after, after_rolled


def advance(S, V0, V1, V2, VN, NR, AIR, DRAG, emit, x):
    sweep_layer(
        lambda k, d, zs: S[k, x + d, :, zs],
        lambda d, zs: V0[x + d, :, zs],
        lambda zs: V1[x - 1, :, zs],
        lambda zs: V2[x - 1, :, zs],
        lambda side, zs: VN[side, x - 1, :, zs],
        lambda side, k, zs: NR[side, k, x - 1, :, zs],
        lambda k, zs: AIR[k, x - 1, :, zs],
        lambda zs: DRAG[x - 1, :, zs],
        emit,
    )


def layer_of(i):
    return jnp.where(i < NX - 2, i + 2, jnp.where(i == NX - 2, 1, NX))


def prepare(owner_ref, face_ref, rank_ref, key8_ref, send_ref, hot_ref, n):
    q_len = 256
    quarters = NZ // q_len
    tri = (iota((q_len, q_len), 0) <= iota((q_len, q_len), 1)).astype(F32).astype(BF16)
    names = iota((OWNERS, q_len), 0)
    mine = n * N_SPAN + iota((N_SPAN, NZ), 0)
    slot = iota((SLOTS, NZ), 0)
    for h in range(2):
        pieces = []
        for b in range(4):
            offset = jnp.zeros((OWNERS, 1), F32)
            got = jnp.zeros((N_SPAN, 2 * SLOTS), F32)
            for half in range(2):
                x = h * 8 + b * 2 + half
                owner = owner_ref[x]
                order = (owner & (N_NORMAL - 1)) * N_SPAN + (owner >> 3)
                hots = []
                for q in range(quarters):
                    qs = slice(q * q_len, (q + 1) * q_len)
                    hot = (order[:, qs] == names).astype(F32).astype(BF16)
                    hot_ref[x, :, qs] = hot
                    hots.append(hot)
                counts = jnp.dot(
                    jnp.concatenate(hots, axis=0), tri, preferred_element_type=F32
                )
                ranks = []
                for q in range(quarters):
                    hot = order[:, q * q_len : (q + 1) * q_len] == names
                    part = counts[q * OWNERS : (q + 1) * OWNERS]
                    ranks.append(
                        jnp.sum(jnp.where(hot, part + offset, 0.0), axis=0, keepdims=True) - 1.0
                    )
                    offset = offset + part[:, q_len - 1 : q_len]
                rank = jnp.concatenate(ranks, axis=1).astype(I32)
                rank_ref[x] = rank
                key = order * SLOTS + rank
                for t in range(CH):
                    key8_ref[x, t : t + 1, :] = key[:, t * LANES : (t + 1) * LANES]
                face = face_ref[x : x + 1, :]
                at = slot == rank
                high = jnp.where(at, (face >> 7).astype(F32), 0.0)
                low = jnp.where(at, (face & 127).astype(F32), 0.0)
                placed = jnp.concatenate([high, low], axis=0).astype(BF16)
                hot16 = (order == mine).astype(F32).astype(BF16)
                got = got + lax.dot_general(hot16, placed, NT, preferred_element_type=F32)
            pieces.append(got[:, :SLOTS] * 128.0 + got[:, SLOTS:])
        send_ref[:, h, :] = jnp.concatenate(pieces, axis=1).astype(I32)


PR = 24
FR = (0, 1, 2)
MS = (3, 4)
MN = (5, 6, 7)
MC = (8, 9)
AN = (10, 11)
DR = (12, 13)
NEAR = (0, 1, 3, 4, 5, 6, 8, 10, 12)
FAR = (0, 3, 5)
STRIP = len(NEAR) + len(FAR)


def flux_of(w, low, high):
    return jnp.where(w > 0, low, high) * w


def wall_strip(pk, vq, q1, wv):
    lane = iota((PR, LANES), 1)
    last_lane, first_lane = lane == LANES - 1, lane == 0

    def tile(ref, i, t):
        return ref[i, :, t * LANES : (t + 1) * LANES]

    def next_tile(ref, i, t):
        here = pltpu.roll(tile(ref, i, t), LANES - 1, 1)
        if t == CH - 1:
            return jnp.where(last_lane, 0.0, here)
        return jnp.where(last_lane, pltpu.roll(tile(ref, i, t + 1), LANES - 1, 1), here)

    def spanwise(f, v):
        flux = flux_of(v + pltpu.roll(v, PR - 1, 0), f, pltpu.roll(f, PR - 1, 0))
        return flux - pltpu.roll(flux, 1, 0)

    def chordwise(ref, i, f, v, v_next, t, before):
        flux = flux_of(v + v_next, f, next_tile(ref, i, t))
        rolled = pltpu.roll(flux, 1, 1)
        if t == 0:
            before = jnp.minimum(v, 0.0) * f
        return flux - jnp.where(first_lane, before, rolled), rolled

    for y in range(3):
        for t in range(CH):
            zs = slice(t * LANES, (t + 1) * LANES)
            scale = half_step / tile(pk, FR[y], t)
            vq[2 + y, :, zs] = tile(pk, MN[y], t) * scale
            if y < 2:
                vq[y, :, zs] = tile(pk, MS[y], t) * scale
                vq[5 + y, :, zs] = tile(pk, MC[y], t) * scale

    before = [None] * 3
    for t in range(CH):
        zs = slice(t * LANES, (t + 1) * LANES)
        v0, v0_1 = tile(vq, 0, t), tile(vq, 1, t)
        v1, v1_1, v1_2 = tile(vq, 2, t), tile(vq, 3, t), tile(vq, 4, t)
        v2, v2_1 = tile(vq, 5, t), tile(vq, 6, t)
        v2_next, v2_1_next = next_tile(vq, 5, t), next_tile(vq, 6, t)
        a0, a1 = tile(pk, FR[0], t), tile(pk, FR[1], t)
        m0, m1, m2 = (tile(pk, i, t) for i in MN)
        w0, w1 = v1 + v1_1, v1_1 + v1_2
        wall = jnp.minimum(v1, 0.0)
        along, before[0] = chordwise(pk, FR[0], a0, v2, v2_next, t, before[0])
        q1[0, :, zs] = (
            a0 - along - spanwise(a0, v0) - (flux_of(w0, a0, a1) - wall * a0)
        )
        between = flux_of(w0, m0, m1)
        along, before[1] = chordwise(pk, MN[0], m0, v2, v2_next, t, before[1])
        q1[1, :, zs] = (
            m0 - along - spanwise(m0, v0) - (between - wall * m0)
            + pseudo_step * tile(pk, DR[0], t) * (a0 * tile(pk, AN[0], t) - m0)
        )
        along, before[2] = chordwise(pk, MN[1], m1, v2_1, v2_1_next, t, before[2])
        q1[2, :, zs] = (
            m1 - along - spanwise(m1, v0_1) - (flux_of(w1, m1, m2) - between)
            + pseudo_step * tile(pk, DR[1], t) * (a1 * tile(pk, AN[1], t) - m1)
        )

    before = None
    for t in range(CH):
        zs = slice(t * LANES, (t + 1) * LANES)
        v0, v1, v1_1, v2 = (tile(vq, i, t) for i in (0, 2, 3, 5))
        a0, m0, m1 = (tile(q1, i, t) for i in range(3))
        along, before = chordwise(q1, 1, m0, v2, next_tile(vq, 5, t), t, before)
        out = (
            m0 - along - spanwise(m0, v0)
            - (flux_of(v1 + v1_1, m0, m1) - jnp.minimum(v1, 0.0) * m0)
            + pseudo_step * tile(pk, DR[0], t) * (a0 * tile(pk, AN[0], t) - m0)
        )
        catch = jnp.maximum(-out, 0.0)
        wv[0, :, zs] = catch
        wv[1, :, zs] = (
            catch * (0.5 / (half_step * half_step)) * (v0 * v0 + v1 * v1 + v2 * v2)
        )


def main_kernel(
    a_hbm, m_hbm, air_hbm, drag_hbm, owner_hbm, face_hbm,
    film_hbm, ice_hbm, cool_hbm, shed_hbm, share_hbm, up_hbm,
    frac_out, mom_out, film_out, ice_out, all_ref, key8_ref,
    owner_ref, face_ref, film_ref, ice_ref, cool_ref, shed_ref, share_ref, up_ref,
    s_ref, s1_ref, v0_ref, v1_ref, v2_ref, vn_ref, ns_ref, nr_ref, nr2_ref, air_ref, drag_ref,
    owner_hot, rank_ref, sendface_ref, pk, vq, q1, wv, strip_out, strip_in,
    slots_ref, fw_ref, part_ref, got_ref, gotface_ref, lhs_ref, hot_ref,
    links_ref, weight_ref, prev_ref, out_ref, back_ref, col_ref,
    load_sem, small_sem, span_send, span_recv, normal_send, normal_recv, strip_send, strip_recv, sends, recvs,
):
    c, n = lax.axis_index("span"), lax.axis_index("normal")
    right, left = (c + 1) % N_SPAN, (c + N_SPAN - 1) % N_SPAN
    on_wall, has_low, has_high = n == 0, n > 0, n < N_NORMAL - 1
    off_wall = has_low
    last_of_column = n == N_NORMAL - 1
    has_next = jnp.logical_or(has_high, c < N_SPAN - 1)
    has_prev = jnp.logical_or(has_low, c > 0)
    next_c, next_n = jnp.where(last_of_column, c + 1, c), jnp.where(last_of_column, 0, n + 1)
    prev_c, prev_n = jnp.where(on_wall, c - 1, c), jnp.where(on_wall, N_NORMAL - 1, n - 1)
    cross_next = jnp.logical_and(last_of_column, c < N_SPAN - 1)
    cross_prev = jnp.logical_and(on_wall, c > 0)

    first_loads = [
        pltpu.make_async_copy(src, dst, small_sem.at[i])
        for i, (src, dst) in enumerate(((owner_hbm, owner_ref), (face_hbm, face_ref)))
    ]
    loads = [
        pltpu.make_async_copy(a_hbm, s_ref.at[0, pl.ds(1, NX)], load_sem.at[0]),
        pltpu.make_async_copy(m_hbm, s_ref.at[pl.ds(1, 3), pl.ds(1, NX)], load_sem.at[1]),
        pltpu.make_async_copy(air_hbm, air_ref, load_sem.at[2]),
        pltpu.make_async_copy(drag_hbm, drag_ref, load_sem.at[3]),
    ] + [
        pltpu.make_async_copy(src, dst, small_sem.at[2 + i])
        for i, (src, dst) in enumerate(
            ((film_hbm, film_ref), (ice_hbm, ice_ref), (cool_hbm, cool_ref), (shed_hbm, shed_ref),
             (share_hbm, share_ref), (up_hbm, up_ref))
        )
    ]
    for load in first_loads + loads:
        load.start()

    barrier = pltpu.get_barrier_semaphore()

    @pl.loop(1, N_SPAN)
    def _(i):
        pl.semaphore_signal(barrier, 1, device_id=((c + i) % N_SPAN, n), device_id_type=MESH)

    @pl.loop(1, N_NORMAL)
    def _(i):
        pl.semaphore_signal(barrier, 1, device_id=(c, (n + i) % N_NORMAL), device_id_type=MESH)

    @pl.when(cross_next)
    def _():
        pl.semaphore_signal(barrier, 1, device_id=(next_c, next_n), device_id_type=MESH)

    @pl.when(cross_prev)
    def _():
        pl.semaphore_signal(barrier, 1, device_id=(prev_c, prev_n), device_id_type=MESH)

    for load in first_loads:
        load.wait()
    prepare(owner_ref, face_ref, rank_ref, key8_ref, sendface_ref, owner_hot, n)
    for load in loads:
        load.wait()

    @pl.when(on_wall)
    def _():
        for i in range(14):
            pk[i, 0:8, :] = jnp.ones((8, NZ), F32)
            pk[i, 16:24, :] = jnp.ones((8, NZ), F32)
        for x in range(NX):
            at = slice(x + 2, x + 3)
            for y in range(3):
                pk[FR[y], at, :] = s_ref[0, x + 1, y : y + 1, :]
                pk[MN[y], at, :] = s_ref[2, x + 1, y : y + 1, :]
                if y < 2:
                    pk[MS[y], at, :] = s_ref[1, x + 1, y : y + 1, :]
                    pk[MC[y], at, :] = s_ref[3, x + 1, y : y + 1, :]
                    pk[AN[y], at, :] = air_ref[1, x, y : y + 1, :]
                    pk[DR[y], at, :] = drag_ref[x, y : y + 1, :]
        for side, near, far in ((0, NX - 1, NX - 2), (1, 0, 1)):
            for j, i in enumerate(NEAR):
                strip_out[side, j] = pk[i, near + 2 : near + 3, :]
            for j, i in enumerate(FAR):
                strip_out[side, len(NEAR) + j] = pk[i, far + 2 : far + 3, :]

    @pl.loop(0, NX)
    def _(x):
        for k in range(4):
            ns_ref[0, 0, k, x] = s_ref[k, x + 1, 0:1, :]
            ns_ref[0, 1, k, x] = s_ref[k, x + 1, NYB - 1 : NYB, :]

    film0 = film_ref[...]
    shed = shed_ref[...]
    out_ref[0] = film0 * shed

    @pl.when(jnp.logical_not(has_prev))
    def _():
        prev_ref[...] = jnp.zeros((2, 8, LANES), F32)

    crossing = jnp.logical_or(cross_next, cross_prev)
    peers = N_SPAN + N_NORMAL - 2

    @pl.when(crossing)
    def _():
        pl.semaphore_wait(barrier, peers + 1)

    @pl.when(jnp.logical_not(crossing))
    def _():
        pl.semaphore_wait(barrier, peers)

    def remote(src, dst, send, recv, device):
        return pltpu.make_async_remote_copy(
            src_ref=src, dst_ref=dst, send_sem=send, recv_sem=recv,
            device_id=device, device_id_type=MESH,
        )

    def await_bytes(ref, sem):
        pltpu.make_async_copy(ref, ref, sem).wait()

    def to_row(src, dst, which):
        @pl.loop(1, N_SPAN)
        def _(i):
            there = (c + i) % N_SPAN
            remote(src.at[there], dst.at[c], sends.at[which], recvs.at[which], (there, n)).start()

    strips = [
        remote(
            strip_out.at[side], strip_in.at[side], strip_send.at[side], strip_recv.at[side],
            (there, n),
        )
        for side, there in ((0, right), (1, left))
    ]

    @pl.when(on_wall)
    def _():
        for copy in strips:
            copy.start()

    def normal_copies(base, dst):
        return (
            remote(ns_ref.at[base, 0], dst.at[1], normal_send.at[2 * base],
                   normal_recv.at[2 * base], (c, n - 1)),
            remote(ns_ref.at[base, 1], dst.at[0], normal_send.at[2 * base + 1],
                   normal_recv.at[2 * base + 1], (c, n + 1)),
        )

    def start_normal(base, dst):
        low, high = normal_copies(base, dst)

        @pl.when(has_low)
        def _():
            low.start()

        @pl.when(has_high)
        def _():
            high.start()

    def wait_normal(base, dst):
        low, high = normal_copies(base, dst)

        @pl.when(has_low)
        def _():
            low.wait_send()
            high.wait_recv()

        @pl.when(has_high)
        def _():
            high.wait_send()
            low.wait_recv()

        @pl.when(jnp.logical_not(has_low))
        def _():
            dst[0] = jnp.zeros(dst.shape[1:], F32)

        @pl.when(jnp.logical_not(has_high))
        def _():
            dst[1] = jnp.zeros(dst.shape[1:], F32)

    def span_copies(src, dst, base):
        return [
            remote(src.at[:, layer], dst.at[:, target], span_send.at[base + i],
                   span_recv.at[base + i], (there, n))
            for i, (there, layer, target) in enumerate(((right, NX, 0), (left, 1, NX + 1)))
        ]

    start_normal(0, nr_ref)
    to_row(sendface_ref, gotface_ref, 0)
    gotface_ref[c] = sendface_ref[c]

    def pass_on(step):
        return remote(out_ref.at[step], prev_ref.at[step], sends.at[1 + step],
                      recvs.at[1 + step], (next_c, next_n))

    @pl.when(has_next)
    def _():
        pass_on(0).start()

    spans = span_copies(s_ref, s_ref, 0)
    for copy in spans:
        copy.start()

    @pl.when(on_wall)
    def _():
        for copy in strips:
            copy.wait()
        for side, near, far in ((0, 1, 0), (1, NX + 2, NX + 3)):
            for j, i in enumerate(NEAR):
                pk[i, near : near + 1, :] = strip_in[side, j]
            for j, i in enumerate(FAR):
                pk[i, far : far + 1, :] = strip_in[side, len(NEAR) + j]
        wall_strip(pk, vq, q1, wv)
        slot = iota((SLOTS, NZ), 0)

        @pl.loop(0, NX // 2)
        def _(b):
            total = jnp.zeros((4 * SLOTS, OWNERS), F32)
            for half in range(2):
                x = b * 2 + half
                at = slot == rank_ref[x]
                rows = []
                for split in range(2):
                    for v in range(2):
                        value = wv[v, pl.ds(x + 2, 1), :]
                        high = value.astype(BF16).astype(F32)
                        rows.append(jnp.where(at, high if split == 0 else value - high, 0.0))
                weights = jnp.concatenate(rows, axis=0).astype(BF16)
                total = total + lax.dot_general(
                    weights, owner_hot[x], NT, preferred_element_type=F32
                )
            both = total[: 2 * SLOTS] + total[2 * SLOTS :]
            spot = pl.ds(pl.multiple_of(b * SLOTS, SLOTS), SLOTS)
            slots_ref[0, spot, :] = both[:SLOTS]
            slots_ref[1, spot, :] = both[SLOTS:]

        for v in range(2):
            for h in range(2):
                fw_ref[:, 2 * v + h, :] = slots_ref[v, h * LANES : (h + 1) * LANES, :].T

        @pl.loop(1, N_NORMAL)
        def _(i):
            remote(fw_ref.at[pl.ds(i * N_SPAN, N_SPAN)], part_ref, sends.at[3], recvs.at[3],
                   (c, i)).start()

        part_ref[...] = fw_ref[0:N_SPAN]
        to_row(part_ref, got_ref, 4)

    @pl.loop(0, NX)
    def _(x):
        scale = half_step / s_ref[0, x + 1]
        v0_ref[x + 1] = s_ref[1, x + 1] * scale
        v1_ref[x] = s_ref[2, x + 1] * scale
        v2_ref[x] = s_ref[3, x + 1] * scale

    for k in range(4):
        for t in range(8):
            links_ref[k, t : t + 1, :] = up_ref[k : k + 1, t * LANES : (t + 1) * LANES]
            weight_ref[k, t : t + 1, :] = share_ref[k : k + 1, t * LANES : (t + 1) * LANES]
    await_bytes(gotface_ref.at[pl.ds(0, N_SPAN - 1)], recvs.at[0])
    lanes_high = iota((LANES, LANES), 0)
    for s in range(2 * N_SPAN):
        face = gotface_ref[s // 2][s % 2 : s % 2 + 1]
        hot_ref[:, s * LANES : (s + 1) * LANES] = (
            (lanes_high == (face & 127)).astype(F32).astype(BF16)
        )
        back_ref[s : s + 1, :] = face

    @pl.when(has_prev)
    def _():
        await_bytes(prev_ref.at[0], recvs.at[1])

    first_face = (c * N_NORMAL + n) * 1024

    def runin(before, own):
        total = jnp.zeros((8, LANES), F32)
        for k in range(4):
            link = links_ref[k]
            spot = link - (first_face - 1024)
            low, high = spot & 127, spot >> 7
            picked = jnp.zeros((8, LANES), F32)
            for j in range(16):
                line = before[j : j + 1] if j < 8 else own[j - 8 : j - 7]
                value = jnp.take_along_axis(
                    jnp.broadcast_to(line, (8, LANES)), low, axis=1, mode="promise_in_bounds"
                )
                picked = jnp.where(high == j, value, picked)
            total = total + weight_ref[k] * jnp.where(link >= 0, picked, 0.0)
        return total

    run0 = runin(prev_ref[0], out_ref[0])

    wait_normal(0, nr_ref)

    def edge_speed(side, present):
        @pl.when(present)
        def _():
            @pl.loop(0, NX)
            def _(x):
                vn_ref[side, x] = nr_ref[side, 2, x] * (half_step / nr_ref[side, 0, x])

        @pl.when(jnp.logical_not(present))
        def _():
            vn_ref[side] = jnp.zeros(vn_ref.shape[1:], F32)

    edge_speed(0, has_low)
    edge_speed(1, has_high)

    def first_layer(i):
        x = layer_of(i)

        def emit(t, zs, acc, v0, v1, v2):
            for k in range(4):
                s1_ref[k, x, :, zs] = acc[k]
                ns_ref[1, 0, k, x - 1, :, zs] = acc[k][0:1]
                ns_ref[1, 1, k, x - 1, :, zs] = acc[k][NYB - 1 : NYB]

        advance(s_ref, v0_ref, v1_ref, v2_ref, vn_ref, nr_ref, air_ref, drag_ref, emit, x)

    @pl.loop(0, FIRST_CUT)
    def _(i):
        first_layer(i)

    @pl.when(off_wall)
    def _():
        await_bytes(part_ref, recvs.at[3])
        to_row(part_ref, got_ref, 4)

    got_ref[c] = part_ref[c]

    @pl.loop(FIRST_CUT, NX)
    def _(i):
        @pl.when(i == NX - 2)
        def _():
            for copy in spans:
                copy.wait()
            for edge in (0, NX + 1):
                v0_ref[edge] = s_ref[1, edge] * (half_step / s_ref[0, edge])

        first_layer(i)

    start_normal(1, nr2_ref)
    again = span_copies(s1_ref, s1_ref, 2)
    for copy in again:
        copy.start()

    await_bytes(got_ref.at[pl.ds(0, N_SPAN - 1)], recvs.at[4])
    eight = iota((8, LANES), 0)
    for s in range(2 * N_SPAN):
        at = eight == (back_ref[s : s + 1, :] >> 7)
        values = [got_ref[s // 2][2 * v + s % 2 : 2 * v + s % 2 + 1] for v in range(2)]
        highs = [value.astype(BF16).astype(F32) for value in values]
        rows = []
        for part in (highs, [values[v] - highs[v] for v in range(2)]):
            rows.extend(jnp.where(at, part[v], 0.0) for v in range(2))
        lhs_ref[:, s * LANES : (s + 1) * LANES] = jnp.concatenate(rows, axis=0).astype(BF16)
    sums = lax.dot_general(lhs_ref[...], hot_ref[...], NT, preferred_element_type=F32)
    sums = sums[:16] + sums[16:]
    face_catch = sums[:8]
    heat = cool_ref[...] / (1.0 + sums[8:])

    def film_step(film, outflow, run):
        inflow = impact_rate * face_catch + film - outflow + run
        frozen = heat * inflow / (heat + inflow)
        return inflow - frozen, frozen

    film1, frozen1 = film_step(film0, out_ref[0], run0)
    out_ref[1] = film1 * shed

    @pl.when(has_next)
    def _():
        pass_on(1).start()

    @pl.when(has_prev)
    def _():
        await_bytes(prev_ref.at[1], recvs.at[2])

    run1 = runin(prev_ref[1], out_ref[1])
    film2, frozen2 = film_step(film1, out_ref[1], run1)
    film_out[...] = film2
    ice2 = ice_ref[...] + frozen1 + frozen2
    ice_out[...] = ice2

    for g in range(4):
        faces = back_ref[g * 8 : g * 8 + 8, :]
        low, high = faces & 127, faces >> 7
        picked = jnp.zeros((8, LANES), F32)
        for j in range(8):
            value = jnp.take_along_axis(
                jnp.broadcast_to(ice2[j : j + 1], (8, LANES)), low, axis=1,
                mode="promise_in_bounds",
            )
            picked = jnp.where(high == j, value, picked)
        for i in range(4):
            col_ref[0, g * 4 + i] = picked[2 * i : 2 * i + 2]
    to_row(col_ref.at[0], col_ref.at[1], 5)
    col_ref[1, c] = col_ref[0, c]

    wait_normal(1, nr2_ref)

    def second_layer(i):
        x = layer_of(i)

        def emit(t, zs, acc, v0, v1, v2):
            frac_out[x - 1, :, zs] = acc[0]
            for k in range(3):
                mom_out[k, x - 1, :, zs] = acc[1 + k]

        advance(s1_ref, v0_ref, v1_ref, v2_ref, vn_ref, nr2_ref, air_ref, drag_ref, emit, x)

    @pl.loop(0, SECOND_CUT)
    def _(i):
        second_layer(i)

    await_bytes(col_ref.at[1, pl.ds(0, N_SPAN - 1)], recvs.at[5])

    @pl.loop(1, N_NORMAL)
    def _(i):
        there = (n + i) % N_NORMAL
        remote(col_ref.at[1], all_ref.at[n], sends.at[6], recvs.at[6], (c, there)).start()

    all_ref[n] = col_ref[1]

    @pl.loop(SECOND_CUT, NX)
    def _(i):
        @pl.when(i == NX - 2)
        def _():
            for copy in again:
                copy.wait()

        second_layer(i)

    await_bytes(all_ref.at[pl.ds(0, N_NORMAL - 1)], recvs.at[6])

    await_bytes(sendface_ref.at[pl.ds(0, N_SPAN - 1)], sends.at[0])

    @pl.when(has_next)
    def _():
        await_bytes(out_ref.at[0], sends.at[1])
        await_bytes(out_ref.at[1], sends.at[2])

    @pl.when(on_wall)
    def _():
        await_bytes(fw_ref.at[pl.ds(0, OWNERS - N_SPAN)], sends.at[3])

    await_bytes(part_ref.at[pl.ds(0, N_SPAN - 1)], sends.at[4])
    await_bytes(col_ref.at[0, pl.ds(0, N_SPAN - 1)], sends.at[5])
    await_bytes(all_ref.at[pl.ds(0, N_NORMAL - 1)], sends.at[6])


FIRST_CUT = 10
SECOND_CUT = 11


def output_kernel(
    frac_ref, mom_ref, film_ref, ice_ref, all_ref, key8_ref,
    frac_out, mom_out, film_out, ice_out, disp_out,
    pick_ref, row_ref, disp_ref, sems,
):
    n = lax.axis_index("normal")
    put_m = pltpu.make_async_copy(mom_ref, mom_out, sems.at[0])
    put_a = pltpu.make_async_copy(frac_ref, frac_out, sems.at[1])
    put_m.start()
    put_a.start()
    film_out[...] = film_ref[...]
    ice_out[...] = ice_ref[...]

    for h in range(2):
        pick_ref[h * LANES : (h + 1) * LANES, :] = (
            all_ref[:, :, h, :].reshape(OWNERS, LANES).T
        )
    y = (n * NYB + iota((NYB, LANES), 0)).astype(F32) + 0.5
    left = 1.0 - y / (NYB * N_NORMAL)
    profile = left * left
    group = 4
    puts = []
    for g in range(NX // group):

        @pl.loop(g * group, (g + 1) * group)
        def _(x):
            key = key8_ref[x]
            order, rank = key >> 5, key & (SLOTS - 1)
            base = pl.multiple_of((x // 2) * SLOTS, SLOTS)
            table = pick_ref[pl.ds(base, SLOTS), :]
            picked = jnp.zeros((8, LANES), F32)
            for j in range(SLOTS):
                value = jnp.take_along_axis(
                    jnp.broadcast_to(table[j : j + 1], (8, LANES)), order, axis=1,
                    mode="promise_in_bounds",
                )
                picked = jnp.where(rank == j, value, picked)
            row_ref[...] = picked
            for t in range(CH):
                disp_ref[x, :, t * LANES : (t + 1) * LANES] = row_ref[t : t + 1, :] * profile

        part = pl.ds(g * group, group)
        put = pltpu.make_async_copy(disp_ref.at[part], disp_out.at[part], sems.at[2 + g])
        put.start()
        puts.append(put)
    put_m.wait()
    put_a.wait()
    for put in puts:
        put.wait()


def shape(dims, dtype=F32):
    return jax.ShapeDtypeStruct(dims, dtype)


VM = pl.BlockSpec(memory_space=pltpu.VMEM)
HBM = pl.BlockSpec(memory_space=pltpu.HBM)


def per_device(
    volume_fraction, droplet_momentum, air_velocity, drag, wall_owner, wall_face,
    film, ice, cooling, shed, share, upstream,
):
    brick = (NX, NYB, NZ)
    tile = (8, LANES)
    rows = (NX, 1, NZ)
    hbm = functools.partial(pltpu.with_memory_space_constraint, memory_space=pltpu.HBM)
    dma = pltpu.SemaphoreType.DMA
    frac, mom, film_now, ice_now, ice_slots, keys = pl.pallas_call(
        main_kernel,
        out_shape=(
            shape(brick), shape((3,) + brick), shape(tile), shape(tile),
            shape((N_NORMAL, N_SPAN, 2, LANES)), shape((NX, 8, LANES), I32),
        ),
        in_specs=[HBM] * 12,
        out_specs=(VM,) * 6,
        scratch_shapes=[
            pltpu.VMEM(rows, I32),
            pltpu.VMEM((NX, NZ), I32),
            pltpu.VMEM(tile, F32),
            pltpu.VMEM(tile, F32),
            pltpu.VMEM(tile, F32),
            pltpu.VMEM(tile, F32),
            pltpu.VMEM((4, NZ), F32),
            pltpu.VMEM((4, NZ), I32),
            pltpu.VMEM((4, NX + 2, NYB, NZ), F32),
            pltpu.VMEM((4, NX + 2, NYB, NZ), F32),
            pltpu.VMEM((NX + 2, NYB, NZ), F32),
            pltpu.VMEM(brick, F32),
            pltpu.VMEM(brick, F32),
            pltpu.VMEM((2,) + rows, F32),
            pltpu.VMEM((2, 2, 4) + rows, F32),
            pltpu.VMEM((2, 4) + rows, F32),
            pltpu.VMEM((2, 4) + rows, F32),
            pltpu.VMEM((3,) + brick, F32),
            pltpu.VMEM(brick, F32),
            pltpu.VMEM((NX, OWNERS, NZ), BF16),
            pltpu.VMEM(rows, I32),
            pltpu.VMEM((N_SPAN, 2, LANES), I32),
            pltpu.VMEM((14, PR, NZ), F32),
            pltpu.VMEM((7, PR, NZ), F32),
            pltpu.VMEM((3, PR, NZ), F32),
            pltpu.VMEM((2, PR, NZ), F32),
            pltpu.VMEM((2, STRIP, 1, NZ), F32),
            pltpu.VMEM((2, STRIP, 1, NZ), F32),
            pltpu.VMEM((2, 8 * SLOTS, OWNERS), F32),
            pltpu.VMEM((OWNERS, 4, LANES), F32),
            pltpu.VMEM((N_SPAN, 4, LANES), F32),
            pltpu.VMEM((N_SPAN, 4, LANES), F32),
            pltpu.VMEM((N_SPAN, 2, LANES), I32),
            pltpu.VMEM((32, 2 * N_SPAN * LANES), BF16),
            pltpu.VMEM((LANES, 2 * N_SPAN * LANES), BF16),
            pltpu.VMEM((4, 8, LANES), I32),
            pltpu.VMEM((4, 8, LANES), F32),
            pltpu.VMEM((2, 8, LANES), F32),
            pltpu.VMEM((2, 8, LANES), F32),
            pltpu.VMEM((2 * N_SPAN, LANES), I32),
            pltpu.VMEM((2, N_SPAN, 2, LANES), F32),
            dma((4,)), dma((8,)), dma((4,)), dma((4,)), dma((4,)), dma((4,)), dma((2,)), dma((2,)),
            dma((7,)), dma((7,)),
        ],
        compiler_params=pltpu.CompilerParams(
            collective_id=0, has_side_effects=True, vmem_limit_bytes=40 * MB
        ),
        name="accretion",
    )(
        *map(
            hbm,
            (
                volume_fraction, droplet_momentum, air_velocity, drag,
                wall_owner.reshape(rows), wall_face,
                film.reshape(tile), ice.reshape(tile), cooling.reshape(tile), shed.reshape(tile),
                share, upstream,
            ),
        )
    )

    fraction_out, momentum_out, film_out, ice_out, displacement = pl.pallas_call(
        output_kernel,
        out_shape=(
            shape(brick), shape((3,) + brick), shape(tile), shape(tile), shape(brick),
        ),
        in_specs=[VM] * 6,
        out_specs=(HBM, HBM, VM, VM, HBM),
        scratch_shapes=[
            pltpu.VMEM((8 * SLOTS, OWNERS), F32),
            pltpu.VMEM((8, LANES), F32),
            pltpu.VMEM(brick, F32),
            dma((6,)),
        ],
        compiler_params=pltpu.CompilerParams(vmem_limit_bytes=32 * MB),
        name="results",
    )(frac, mom, film_now, ice_now, ice_slots, keys)
    return fraction_out, momentum_out, film_out.reshape(-1), ice_out.reshape(-1), displacement


def solution(mesh):
    volume = P("span", "normal", None)
    vector = P(None, "span", "normal", None)
    faces = P(("span", "normal"))
    links = P(None, ("span", "normal"))
    return jax.shard_map(
        per_device,
        mesh=mesh,
        in_specs=(
            volume, vector, vector, volume, P("span", None, None), P("span", None),
            faces, faces, faces, faces, links, links,
        ),
        out_specs=(volume, vector, faces, faces, volume),
        check_vma=False,
    )
```

```python
import functools

import jax
import jax.numpy as jnp
from jax import lax
from jax.experimental import pallas as pl
from jax.experimental.pallas import tpu as pltpu
from jax.sharding import PartitionSpec as P

F32 = jnp.float32
BF16 = jnp.bfloat16
I32 = jnp.int32
MESH = pl.DeviceIdType.MESH
pseudo_step = 0.15
impact_rate = 4.0
half_step = 0.5 * pseudo_step
NX = 16
NYB = 16
NZ = 1024
LANES = 128
CH = NZ // LANES
N_SPAN = 16
N_NORMAL = 8
OWNERS = N_SPAN * N_NORMAL
SLOTS = 32
MB = 1 << 20
NT = (((1,), (1,)), ((), ()))


def iota(shape, dim):
    return lax.broadcasted_iota(I32, shape, dim)


def sweep_layer(S, V0, V1, V2, VN, NR, AIR, DRAG, emit):
    lane = iota((NYB, LANES), 1)
    row = iota((NYB, LANES), 0)
    last_lane, first_lane = lane == LANES - 1, lane == 0
    last_row, first_row = row == NYB - 1, row == 0

    def chord(c):
        zs = pl.ds(c * LANES, LANES)
        return [S(k, 0, zs) for k in range(4)] + [V2(zs)]

    here = chord(0)
    here_rolled = [pltpu.roll(t, LANES - 1, 1) for t in here]
    before = None
    for c in range(CH):
        zs = pl.ds(c * LANES, LANES)
        if c < CH - 1:
            after = chord(c + 1)
            after_rolled = [pltpu.roll(t, LANES - 1, 1) for t in after]
        else:
            after = after_rolled = [jnp.zeros((NYB, LANES), F32)] * 5
        f, v2 = here[:4], here[4]
        up = [jnp.where(last_lane, after_rolled[i], here_rolled[i]) for i in range(5)]
        w = v2 + up[4]
        pos = w > 0
        flux = [jnp.where(pos, f[k], up[k]) * w for k in range(4)]
        rolled = [pltpu.roll(t, 1, 1) for t in flux]
        if c == 0:
            edge = jnp.minimum(v2, 0.0)
            before = [edge * f[k] for k in range(4)]
        acc = [f[k] - (flux[k] - jnp.where(first_lane, before[k], rolled[k])) for k in range(4)]
        before = rolled

        v1 = V1(zs)
        w = v1 + jnp.where(last_row, VN(1, zs), pltpu.roll(v1, NYB - 1, 0))
        pos = w > 0
        w_low = VN(0, zs) + v1[0:1]
        pos_low = w_low > 0
        for k in range(4):
            upper = jnp.where(last_row, NR(1, k, zs), pltpu.roll(f[k], NYB - 1, 0))
            flux_k = jnp.where(pos, f[k], upper) * w
            low = jnp.where(pos_low, NR(0, k, zs), f[k][0:1]) * w_low
            acc[k] = acc[k] - (flux_k - jnp.where(first_row, low, pltpu.roll(flux_k, 1, 0)))

        v0 = V0(0, zs)
        w = v0 + V0(1, zs)
        w_low = V0(-1, zs) + v0
        pos, pos_low = w > 0, w_low > 0
        for k in range(4):
            flux_k = jnp.where(pos, f[k], S(k, 1, zs)) * w
            low = jnp.where(pos_low, S(k, -1, zs), f[k]) * w_low
            acc[k] = acc[k] - (flux_k - low)

        pull = pseudo_step * DRAG(zs)
        for k in range(3):
            acc[1 + k] = acc[1 + k] + pull * (f[0] * AIR(k, zs) - f[1 + k])
        emit(c, zs, acc, v0, v1, v2)
        here, here_rolled = after, after_rolled


def advance(S, V0, V1, V2, VN, NR, AIR, DRAG, emit, x):
    sweep_layer(
        lambda k, d, zs: S[k, x + d, :, zs],
        lambda d, zs: V0[x + d, :, zs],
        lambda zs: V1[x - 1, :, zs],
        lambda zs: V2[x - 1, :, zs],
        lambda side, zs: VN[side, x - 1, :, zs],
        lambda side, k, zs: NR[side, k, x - 1, :, zs],
        lambda k, zs: AIR[k, x - 1, :, zs],
        lambda zs: DRAG[x - 1, :, zs],
        emit,
    )


def layer_of(i):
    return jnp.where(i < NX - 2, i + 2, jnp.where(i == NX - 2, 1, NX))


def prepare(owner_ref, face_ref, rank_ref, key8_ref, send_ref, hot_ref, n, h):
    q_len = 256
    quarters = NZ // q_len
    tri = (iota((q_len, q_len), 0) <= iota((q_len, q_len), 1)).astype(F32).astype(BF16)
    names = iota((OWNERS, q_len), 0)
    mine = n * N_SPAN + iota((N_SPAN, NZ), 0)
    slot = iota((SLOTS, NZ), 0)
    pieces = []
    for b in range(4):
        offset = jnp.zeros((OWNERS, 1), F32)
        got = jnp.zeros((N_SPAN, 2 * SLOTS), F32)
        for half in range(2):
            x = h * 8 + b * 2 + half
            owner = owner_ref[x]
            order = (owner & (N_NORMAL - 1)) * N_SPAN + (owner >> 3)
            hots = []
            for q in range(quarters):
                qs = slice(q * q_len, (q + 1) * q_len)
                hot = (order[:, qs] == names).astype(F32).astype(BF16)
                hot_ref[x, :, qs] = hot
                hots.append(hot)
            counts = jnp.dot(
                jnp.concatenate(hots, axis=0), tri, preferred_element_type=F32
            )
            ranks = []
            for q in range(quarters):
                part = counts[q * OWNERS : (q + 1) * OWNERS]
                ranks.append(
                    jnp.sum(hots[q].astype(F32) * (part + offset), axis=0, keepdims=True) - 1.0
                )
                offset = offset + part[:, q_len - 1 : q_len]
            rank = jnp.concatenate(ranks, axis=1).astype(I32)
            rank_ref[x] = rank
            key = order * SLOTS + rank
            for t in range(CH):
                key8_ref[x, t : t + 1, :] = key[:, t * LANES : (t + 1) * LANES]
            face = face_ref[x : x + 1, :]
            at = slot == rank
            high = jnp.where(at, (face >> 7).astype(F32), 0.0)
            low = jnp.where(at, (face & 127).astype(F32), 0.0)
            placed = jnp.concatenate([high, low], axis=0).astype(BF16)
            hot16 = (order == mine).astype(F32).astype(BF16)
            got = got + lax.dot_general(hot16, placed, NT, preferred_element_type=F32)
        pieces.append(got[:, :SLOTS] * 128.0 + got[:, SLOTS:])
    send_ref[:, h, :] = jnp.concatenate(pieces, axis=1).astype(I32)


PR = 24
FR = (0, 1, 2)
MS = (3, 4)
MN = (5, 6, 7)
MC = (8, 9)
AN = (10, 11)
DR = (12, 13)
NEAR = (0, 1, 3, 4, 5, 6, 8, 10, 12)
FAR = (0, 3, 5)
STRIP = len(NEAR) + len(FAR)


def flux_of(w, low, high):
    return jnp.where(w > 0, low, high) * w


def wall_strip(pk, vq, q1, wv):
    lane = iota((PR, LANES), 1)
    last_lane, first_lane = lane == LANES - 1, lane == 0

    def tile(ref, i, t):
        return ref[i, :, t * LANES : (t + 1) * LANES]

    def next_tile(ref, i, t):
        here = pltpu.roll(tile(ref, i, t), LANES - 1, 1)
        if t == CH - 1:
            return jnp.where(last_lane, 0.0, here)
        return jnp.where(last_lane, pltpu.roll(tile(ref, i, t + 1), LANES - 1, 1), here)

    def spanwise(f, v):
        flux = flux_of(v + pltpu.roll(v, PR - 1, 0), f, pltpu.roll(f, PR - 1, 0))
        return flux - pltpu.roll(flux, 1, 0)

    def chordwise(ref, i, f, v, v_next, t, before):
        flux = flux_of(v + v_next, f, next_tile(ref, i, t))
        rolled = pltpu.roll(flux, 1, 1)
        if t == 0:
            before = jnp.minimum(v, 0.0) * f
        return flux - jnp.where(first_lane, before, rolled), rolled

    for y in range(3):
        for t in range(CH):
            zs = slice(t * LANES, (t + 1) * LANES)
            scale = half_step / tile(pk, FR[y], t)
            vq[2 + y, :, zs] = tile(pk, MN[y], t) * scale
            if y < 2:
                vq[y, :, zs] = tile(pk, MS[y], t) * scale
                vq[5 + y, :, zs] = tile(pk, MC[y], t) * scale

    before = [None] * 3
    for t in range(CH):
        zs = slice(t * LANES, (t + 1) * LANES)
        v0, v0_1 = tile(vq, 0, t), tile(vq, 1, t)
        v1, v1_1, v1_2 = tile(vq, 2, t), tile(vq, 3, t), tile(vq, 4, t)
        v2, v2_1 = tile(vq, 5, t), tile(vq, 6, t)
        v2_next, v2_1_next = next_tile(vq, 5, t), next_tile(vq, 6, t)
        a0, a1 = tile(pk, FR[0], t), tile(pk, FR[1], t)
        m0, m1, m2 = (tile(pk, i, t) for i in MN)
        w0, w1 = v1 + v1_1, v1_1 + v1_2
        wall = jnp.minimum(v1, 0.0)
        along, before[0] = chordwise(pk, FR[0], a0, v2, v2_next, t, before[0])
        q1[0, :, zs] = (
            a0 - along - spanwise(a0, v0) - (flux_of(w0, a0, a1) - wall * a0)
        )
        between = flux_of(w0, m0, m1)
        along, before[1] = chordwise(pk, MN[0], m0, v2, v2_next, t, before[1])
        q1[1, :, zs] = (
            m0 - along - spanwise(m0, v0) - (between - wall * m0)
            + pseudo_step * tile(pk, DR[0], t) * (a0 * tile(pk, AN[0], t) - m0)
        )
        along, before[2] = chordwise(pk, MN[1], m1, v2_1, v2_1_next, t, before[2])
        q1[2, :, zs] = (
            m1 - along - spanwise(m1, v0_1) - (flux_of(w1, m1, m2) - between)
            + pseudo_step * tile(pk, DR[1], t) * (a1 * tile(pk, AN[1], t) - m1)
        )

    before = None
    for t in range(CH):
        zs = slice(t * LANES, (t + 1) * LANES)
        v0, v1, v1_1, v2 = (tile(vq, i, t) for i in (0, 2, 3, 5))
        a0, m0, m1 = (tile(q1, i, t) for i in range(3))
        along, before = chordwise(q1, 1, m0, v2, next_tile(vq, 5, t), t, before)
        out = (
            m0 - along - spanwise(m0, v0)
            - (flux_of(v1 + v1_1, m0, m1) - jnp.minimum(v1, 0.0) * m0)
            + pseudo_step * tile(pk, DR[0], t) * (a0 * tile(pk, AN[0], t) - m0)
        )
        catch = jnp.maximum(-out, 0.0)
        wv[0, :, zs] = catch
        wv[1, :, zs] = (
            catch * (0.5 / (half_step * half_step)) * (v0 * v0 + v1 * v1 + v2 * v2)
        )


def main_kernel(
    a_hbm, m_hbm, air_hbm, drag_hbm, owner_hbm, face_hbm,
    film_hbm, ice_hbm, cool_hbm, shed_hbm, share_hbm, up_hbm,
    frac_out, mom_out, film_out, ice_out, all_ref, key8_ref,
    owner_ref, face_ref, film_ref, ice_ref, cool_ref, shed_ref, share_ref, up_ref,
    s_ref, s1_ref, v0_ref, v1_ref, v2_ref, vn_ref, ns_ref, nr_ref, nr2_ref, air_ref, drag_ref,
    owner_hot, rank_ref, sendface_ref, pk, vq, q1, wv, strip_out, strip_in,
    slots_ref, fw_ref, part_ref, got_ref, gotface_ref, lhs_ref, hot_ref,
    links_ref, weight_ref, prev_ref, out_ref, back_ref, col_ref,
    load_sem, small_sem, span_send, span_recv, normal_send, normal_recv, strip_send, strip_recv, sends, recvs,
):
    c, n = lax.axis_index("span"), lax.axis_index("normal")
    right, left = (c + 1) % N_SPAN, (c + N_SPAN - 1) % N_SPAN
    on_wall, has_low, has_high = n == 0, n > 0, n < N_NORMAL - 1
    off_wall = has_low
    last_of_column = n == N_NORMAL - 1
    has_next = jnp.logical_or(has_high, c < N_SPAN - 1)
    has_prev = jnp.logical_or(has_low, c > 0)
    next_c, next_n = jnp.where(last_of_column, c + 1, c), jnp.where(last_of_column, 0, n + 1)
    prev_c, prev_n = jnp.where(on_wall, c - 1, c), jnp.where(on_wall, N_NORMAL - 1, n - 1)
    cross_next = jnp.logical_and(last_of_column, c < N_SPAN - 1)
    cross_prev = jnp.logical_and(on_wall, c > 0)

    first_loads = [
        pltpu.make_async_copy(src, dst, small_sem.at[i])
        for i, (src, dst) in enumerate(((owner_hbm, owner_ref), (face_hbm, face_ref)))
    ]
    low, high = pl.ds(0, 8), pl.ds(8, 8)
    whole = pl.ds(1, NX)
    low_loads = [
        pltpu.make_async_copy(src, dst, load_sem.at[i])
        for i, (src, dst) in enumerate(
            (
                (a_hbm.at[:, low], s_ref.at[0, whole, low]),
                (m_hbm.at[:, :, low], s_ref.at[pl.ds(1, 3), whole, low]),
                (air_hbm.at[1, :, low], air_ref.at[1, :, low]),
                (drag_hbm.at[:, low], drag_ref.at[:, low]),
            )
        )
    ]
    loads = [
        pltpu.make_async_copy(src, dst, load_sem.at[4 + i])
        for i, (src, dst) in enumerate(
            (
                (a_hbm.at[:, high], s_ref.at[0, whole, high]),
                (m_hbm.at[:, :, high], s_ref.at[pl.ds(1, 3), whole, high]),
                (air_hbm.at[1, :, high], air_ref.at[1, :, high]),
                (drag_hbm.at[:, high], drag_ref.at[:, high]),
                (air_hbm.at[0], air_ref.at[0]),
                (air_hbm.at[2], air_ref.at[2]),
            )
        )
    ] + [
        pltpu.make_async_copy(src, dst, small_sem.at[2 + i])
        for i, (src, dst) in enumerate(
            ((film_hbm, film_ref), (ice_hbm, ice_ref), (cool_hbm, cool_ref), (shed_hbm, shed_ref),
             (share_hbm, share_ref), (up_hbm, up_ref))
        )
    ]
    for load in first_loads + low_loads + loads:
        load.start()

    barrier = pltpu.get_barrier_semaphore()

    @pl.loop(1, N_SPAN)
    def _(i):
        pl.semaphore_signal(barrier, 1, device_id=((c + i) % N_SPAN, n), device_id_type=MESH)

    @pl.loop(1, N_NORMAL)
    def _(i):
        pl.semaphore_signal(barrier, 1, device_id=(c, (n + i) % N_NORMAL), device_id_type=MESH)

    @pl.when(cross_next)
    def _():
        pl.semaphore_signal(barrier, 1, device_id=(next_c, next_n), device_id_type=MESH)

    @pl.when(cross_prev)
    def _():
        pl.semaphore_signal(barrier, 1, device_id=(prev_c, prev_n), device_id_type=MESH)

    for load in first_loads:
        load.wait()
    prepare(owner_ref, face_ref, rank_ref, key8_ref, sendface_ref, owner_hot, n, 0)
    for load in low_loads:
        load.wait()

    def packed_row(i, x):
        if i in FR:
            return s_ref[0, x + 1, FR.index(i) : FR.index(i) + 1, :]
        for k, sets in ((1, MS), (2, MN), (3, MC)):
            if i in sets:
                y = sets.index(i)
                return s_ref[k, x + 1, y : y + 1, :]
        if i in AN:
            return air_ref[1, x, AN.index(i) : AN.index(i) + 1, :]
        return drag_ref[x, DR.index(i) : DR.index(i) + 1, :]

    @pl.when(on_wall)
    def _():
        for side, near, far in ((0, NX - 1, NX - 2), (1, 0, 1)):
            for j, i in enumerate(NEAR):
                strip_out[side, j] = packed_row(i, near)
            for j, i in enumerate(FAR):
                strip_out[side, len(NEAR) + j] = packed_row(i, far)

    @pl.when(jnp.logical_not(has_prev))
    def _():
        prev_ref[...] = jnp.zeros((2, 8, LANES), F32)

    crossing = jnp.logical_or(cross_next, cross_prev)
    peers = N_SPAN + N_NORMAL - 2

    @pl.when(crossing)
    def _():
        pl.semaphore_wait(barrier, peers + 1)

    @pl.when(jnp.logical_not(crossing))
    def _():
        pl.semaphore_wait(barrier, peers)

    def remote(src, dst, send, recv, device):
        return pltpu.make_async_remote_copy(
            src_ref=src, dst_ref=dst, send_sem=send, recv_sem=recv,
            device_id=device, device_id_type=MESH,
        )

    def await_bytes(ref, sem):
        pltpu.make_async_copy(ref, ref, sem).wait()

    def far_first(place, i):
        return (place + jnp.where(i == 3, 0, jnp.where(i == 0, 2, 2 * i - 1))) & 3

    def row_peer(i):
        return far_first(c >> 2, i >> 2) * 4 + far_first(c & 3, i & 3)

    def to_row(src, dst, which):
        @pl.loop(0, N_SPAN - 1)
        def _(i):
            there = row_peer(i)
            remote(src.at[there], dst.at[c], sends.at[which], recvs.at[which], (there, n)).start()

    strips = [
        remote(
            strip_out.at[side], strip_in.at[side], strip_send.at[side], strip_recv.at[side],
            (there, n),
        )
        for side, there in ((0, right), (1, left))
    ]

    @pl.when(on_wall)
    def _():
        for copy in strips:
            copy.start()

    def normal_copies(base, dst):
        return (
            remote(ns_ref.at[base, 0], dst.at[1], normal_send.at[2 * base],
                   normal_recv.at[2 * base], (c, n - 1)),
            remote(ns_ref.at[base, 1], dst.at[0], normal_send.at[2 * base + 1],
                   normal_recv.at[2 * base + 1], (c, n + 1)),
        )

    def start_normal(base, dst):
        low, high = normal_copies(base, dst)

        @pl.when(has_low)
        def _():
            low.start()

        @pl.when(has_high)
        def _():
            high.start()

    def wait_normal(base, dst):
        low, high = normal_copies(base, dst)

        @pl.when(has_low)
        def _():
            low.wait_send()
            high.wait_recv()

        @pl.when(has_high)
        def _():
            high.wait_send()
            low.wait_recv()

        @pl.when(jnp.logical_not(has_low))
        def _():
            dst[0] = jnp.zeros(dst.shape[1:], F32)

        @pl.when(jnp.logical_not(has_high))
        def _():
            dst[1] = jnp.zeros(dst.shape[1:], F32)

    def span_copies(src, dst, base):
        return [
            remote(src.at[:, layer], dst.at[:, target], span_send.at[base + i],
                   span_recv.at[base + i], (there, n))
            for i, (there, layer, target) in enumerate(((right, NX, 0), (left, 1, NX + 1)))
        ]

    for load in loads:
        load.wait()

    @pl.loop(0, NX)
    def _(x):
        for k in range(4):
            ns_ref[0, 0, k, x] = s_ref[k, x + 1, 0:1, :]
            ns_ref[0, 1, k, x] = s_ref[k, x + 1, NYB - 1 : NYB, :]

    start_normal(0, nr_ref)
    spans = span_copies(s_ref, s_ref, 0)
    for copy in spans:
        copy.start()
    film0 = film_ref[...]
    shed = shed_ref[...]
    out_ref[0] = film0 * shed

    def pass_on(step):
        return remote(out_ref.at[step], prev_ref.at[step], sends.at[1 + step],
                      recvs.at[1 + step], (next_c, next_n))

    @pl.when(has_next)
    def _():
        pass_on(0).start()

    prepare(owner_ref, face_ref, rank_ref, key8_ref, sendface_ref, owner_hot, n, 1)
    to_row(sendface_ref, gotface_ref, 0)
    gotface_ref[c] = sendface_ref[c]

    @pl.loop(0, NX)
    def _(x):
        scale = half_step / s_ref[0, x + 1]
        v0_ref[x + 1] = s_ref[1, x + 1] * scale
        v1_ref[x] = s_ref[2, x + 1] * scale
        v2_ref[x] = s_ref[3, x + 1] * scale

    @pl.when(on_wall)
    def _():
        for i in range(14):
            pk[i, 0:8, :] = jnp.ones((8, NZ), F32)
            pk[i, 16:24, :] = jnp.ones((8, NZ), F32)
        for x in range(NX):
            for i in range(14):
                pk[i, x + 2 : x + 3, :] = packed_row(i, x)
        for copy in strips:
            copy.wait()
        for side, near, far in ((0, 1, 0), (1, NX + 2, NX + 3)):
            for j, i in enumerate(NEAR):
                pk[i, near : near + 1, :] = strip_in[side, j]
            for j, i in enumerate(FAR):
                pk[i, far : far + 1, :] = strip_in[side, len(NEAR) + j]
        wall_strip(pk, vq, q1, wv)
        slot = iota((SLOTS, NZ), 0)

        @pl.loop(0, NX // 2, unroll=2)
        def _(b):
            total = jnp.zeros((4 * SLOTS, OWNERS), F32)
            for half in range(2):
                x = b * 2 + half
                at = slot == rank_ref[x]
                rows = []
                for split in range(2):
                    for v in range(2):
                        value = wv[v, pl.ds(x + 2, 1), :]
                        high = value.astype(BF16).astype(F32)
                        rows.append(jnp.where(at, high if split == 0 else value - high, 0.0))
                weights = jnp.concatenate(rows, axis=0).astype(BF16)
                total = total + lax.dot_general(
                    weights, owner_hot[x], NT, preferred_element_type=F32
                )
            both = total[: 2 * SLOTS] + total[2 * SLOTS :]
            spot = pl.ds(pl.multiple_of(b * SLOTS, SLOTS), SLOTS)
            slots_ref[0, spot, :] = both[:SLOTS]
            slots_ref[1, spot, :] = both[SLOTS:]

        for v in range(2):
            for h in range(2):
                fw_ref[:, 2 * v + h, :] = slots_ref[v, h * LANES : (h + 1) * LANES, :].T

        @pl.loop(0, N_NORMAL - 1)
        def _(i):
            there = 2 * far_first(0, i >> 1) + 1 - (i & 1)
            remote(fw_ref.at[pl.ds(there * N_SPAN, N_SPAN)], part_ref, sends.at[3], recvs.at[3],
                   (c, there)).start()

        part_ref[...] = fw_ref[0:N_SPAN]
        to_row(part_ref, got_ref, 4)

    for k in range(4):
        for t in range(8):
            links_ref[k, t : t + 1, :] = up_ref[k : k + 1, t * LANES : (t + 1) * LANES]
            weight_ref[k, t : t + 1, :] = share_ref[k : k + 1, t * LANES : (t + 1) * LANES]
    await_bytes(gotface_ref.at[pl.ds(0, N_SPAN - 1)], recvs.at[0])
    lanes_high = iota((LANES, LANES), 0)
    for s in range(2 * N_SPAN):
        face = gotface_ref[s // 2][s % 2 : s % 2 + 1]
        hot_ref[:, s * LANES : (s + 1) * LANES] = (
            (lanes_high == (face & 127)).astype(F32).astype(BF16)
        )
        back_ref[s : s + 1, :] = face

    @pl.when(has_prev)
    def _():
        await_bytes(prev_ref.at[0], recvs.at[1])

    first_face = (c * N_NORMAL + n) * 1024

    def runin(before, own):
        total = jnp.zeros((8, LANES), F32)
        for k in range(4):
            link = links_ref[k]
            spot = link - (first_face - 1024)
            low, high = spot & 127, spot >> 7
            picked = jnp.zeros((8, LANES), F32)
            for j in range(16):
                line = before[j : j + 1] if j < 8 else own[j - 8 : j - 7]
                value = jnp.take_along_axis(
                    jnp.broadcast_to(line, (8, LANES)), low, axis=1, mode="promise_in_bounds"
                )
                picked = jnp.where(high == j, value, picked)
            total = total + weight_ref[k] * jnp.where(link >= 0, picked, 0.0)
        return total

    run0 = runin(prev_ref[0], out_ref[0])

    wait_normal(0, nr_ref)

    def edge_speed(side, present):
        @pl.when(present)
        def _():
            @pl.loop(0, NX)
            def _(x):
                vn_ref[side, x] = nr_ref[side, 2, x] * (half_step / nr_ref[side, 0, x])

        @pl.when(jnp.logical_not(present))
        def _():
            vn_ref[side] = jnp.zeros(vn_ref.shape[1:], F32)

    edge_speed(0, has_low)
    edge_speed(1, has_high)

    def first_layer(i):
        x = layer_of(i)

        def emit(t, zs, acc, v0, v1, v2):
            for k in range(4):
                s1_ref[k, x, :, zs] = acc[k]
                ns_ref[1, 0, k, x - 1, :, zs] = acc[k][0:1]
                ns_ref[1, 1, k, x - 1, :, zs] = acc[k][NYB - 1 : NYB]

        advance(s_ref, v0_ref, v1_ref, v2_ref, vn_ref, nr_ref, air_ref, drag_ref, emit, x)

    @pl.loop(0, FIRST_CUT)
    def _(i):
        first_layer(i)

    @pl.when(off_wall)
    def _():
        await_bytes(part_ref, recvs.at[3])
        to_row(part_ref, got_ref, 4)

    got_ref[c] = part_ref[c]

    @pl.loop(FIRST_CUT, NX)
    def _(i):
        @pl.when(i == NX - 2)
        def _():
            for copy in spans:
                copy.wait()
            for edge in (0, NX + 1):
                v0_ref[edge] = s_ref[1, edge] * (half_step / s_ref[0, edge])

        first_layer(i)

    start_normal(1, nr2_ref)
    again = span_copies(s1_ref, s1_ref, 2)
    for copy in again:
        copy.start()

    await_bytes(got_ref.at[pl.ds(0, N_SPAN - 1)], recvs.at[4])
    eight = iota((8, LANES), 0)
    for s in range(2 * N_SPAN):
        at = eight == (back_ref[s : s + 1, :] >> 7)
        values = [got_ref[s // 2][2 * v + s % 2 : 2 * v + s % 2 + 1] for v in range(2)]
        highs = [value.astype(BF16).astype(F32) for value in values]
        rows = []
        for part in (highs, [values[v] - highs[v] for v in range(2)]):
            rows.extend(jnp.where(at, part[v], 0.0) for v in range(2))
        lhs_ref[:, s * LANES : (s + 1) * LANES] = jnp.concatenate(rows, axis=0).astype(BF16)
    sums = lax.dot_general(lhs_ref[...], hot_ref[...], NT, preferred_element_type=F32)
    sums = sums[:16] + sums[16:]
    face_catch = sums[:8]
    heat = cool_ref[...] / (1.0 + sums[8:])

    def film_step(film, outflow, run):
        inflow = impact_rate * face_catch + film - outflow + run
        frozen = heat * inflow / (heat + inflow)
        return inflow - frozen, frozen

    film1, frozen1 = film_step(film0, out_ref[0], run0)
    out_ref[1] = film1 * shed

    @pl.when(has_next)
    def _():
        pass_on(1).start()

    @pl.when(has_prev)
    def _():
        await_bytes(prev_ref.at[1], recvs.at[2])

    run1 = runin(prev_ref[1], out_ref[1])
    film2, frozen2 = film_step(film1, out_ref[1], run1)
    film_out[...] = film2
    ice2 = ice_ref[...] + frozen1 + frozen2
    ice_out[...] = ice2

    for g in range(4):
        faces = back_ref[g * 8 : g * 8 + 8, :]
        low, high = faces & 127, faces >> 7
        picked = jnp.zeros((8, LANES), F32)
        for j in range(8):
            value = jnp.take_along_axis(
                jnp.broadcast_to(ice2[j : j + 1], (8, LANES)), low, axis=1,
                mode="promise_in_bounds",
            )
            picked = jnp.where(high == j, value, picked)
        for i in range(4):
            col_ref[g * 4 + i] = picked[2 * i : 2 * i + 2]

    @pl.loop(0, OWNERS - 1)
    def _(i):
        there = row_peer(i >> 3)
        side = 2 * far_first(n >> 1, (i >> 1) & 3) + ((n + 1 + i) & 1)
        remote(col_ref.at[there], all_ref.at[n * N_SPAN + c], sends.at[5], recvs.at[5],
               (there, side)).start()

    all_ref[n * N_SPAN + c] = col_ref[c]

    wait_normal(1, nr2_ref)

    def second_layer(i):
        x = layer_of(i)

        def emit(t, zs, acc, v0, v1, v2):
            frac_out[x - 1, :, zs] = acc[0]
            for k in range(3):
                mom_out[k, x - 1, :, zs] = acc[1 + k]

        advance(s1_ref, v0_ref, v1_ref, v2_ref, vn_ref, nr2_ref, air_ref, drag_ref, emit, x)

    @pl.loop(0, NX)
    def _(i):
        @pl.when(i == NX - 2)
        def _():
            for copy in again:
                copy.wait()

        second_layer(i)

    await_bytes(all_ref.at[pl.ds(0, OWNERS - 1)], recvs.at[5])

    await_bytes(sendface_ref.at[pl.ds(0, N_SPAN - 1)], sends.at[0])

    @pl.when(has_next)
    def _():
        await_bytes(out_ref.at[0], sends.at[1])
        await_bytes(out_ref.at[1], sends.at[2])

    @pl.when(on_wall)
    def _():
        await_bytes(fw_ref.at[pl.ds(0, OWNERS - N_SPAN)], sends.at[3])

    await_bytes(part_ref.at[pl.ds(0, N_SPAN - 1)], sends.at[4])
    await_bytes(all_ref.at[pl.ds(0, OWNERS - 1)], sends.at[5])


FIRST_CUT = 10


def output_kernel(
    frac_ref, mom_ref, film_ref, ice_ref, all_ref, key8_ref,
    frac_out, mom_out, film_out, ice_out, disp_out,
    pick_ref, row_ref, disp_ref, sems,
):
    n = lax.axis_index("normal")
    put_m = pltpu.make_async_copy(mom_ref, mom_out, sems.at[0])
    put_a = pltpu.make_async_copy(frac_ref, frac_out, sems.at[1])
    put_m.start()
    put_a.start()
    put_film = pltpu.make_async_copy(film_ref, film_out, sems.at[6])
    put_ice = pltpu.make_async_copy(ice_ref, ice_out, sems.at[7])
    put_film.start()
    put_ice.start()

    for h in range(2):
        pick_ref[h * LANES : (h + 1) * LANES, :] = (
            all_ref[:, h, :].T
        )
    y = (n * NYB + iota((NYB, LANES), 0)).astype(F32) + 0.5
    left = 1.0 - y / (NYB * N_NORMAL)
    profile = left * left
    group = 4
    puts = []
    for g in range(NX // group):

        @pl.loop(g * group, (g + 1) * group)
        def _(x):
            key = key8_ref[x]
            order, rank = key >> 5, key & (SLOTS - 1)
            base = pl.multiple_of((x // 2) * SLOTS, SLOTS)
            table = pick_ref[pl.ds(base, SLOTS), :]
            picked = jnp.zeros((8, LANES), F32)
            for j in range(SLOTS):
                value = jnp.take_along_axis(
                    jnp.broadcast_to(table[j : j + 1], (8, LANES)), order, axis=1,
                    mode="promise_in_bounds",
                )
                picked = jnp.where(rank == j, value, picked)
            row_ref[...] = picked
            for t in range(CH):
                disp_ref[x, :, t * LANES : (t + 1) * LANES] = row_ref[t : t + 1, :] * profile

        part = pl.ds(g * group, group)
        put = pltpu.make_async_copy(disp_ref.at[part], disp_out.at[part], sems.at[2 + g])
        put.start()
        puts.append(put)
    for put in (put_m, put_a, put_film, put_ice):
        put.wait()
    for put in puts:
        put.wait()


def shape(dims, dtype=F32):
    return jax.ShapeDtypeStruct(dims, dtype)


VM = pl.BlockSpec(memory_space=pltpu.VMEM)
HBM = pl.BlockSpec(memory_space=pltpu.HBM)


def per_device(
    volume_fraction, droplet_momentum, air_velocity, drag, wall_owner, wall_face,
    film, ice, cooling, shed, share, upstream,
):
    brick = (NX, NYB, NZ)
    tile = (8, LANES)
    rows = (NX, 1, NZ)
    hbm = functools.partial(pltpu.with_memory_space_constraint, memory_space=pltpu.HBM)
    dma = pltpu.SemaphoreType.DMA
    frac, mom, film_now, ice_now, ice_slots, keys = pl.pallas_call(
        main_kernel,
        out_shape=(
            shape(brick), shape((3,) + brick), shape(tile), shape(tile),
            shape((OWNERS, 2, LANES)), shape((NX, 8, LANES), I32),
        ),
        in_specs=[HBM] * 12,
        out_specs=(VM,) * 6,
        scratch_shapes=[
            pltpu.VMEM(rows, I32),
            pltpu.VMEM((NX, NZ), I32),
            pltpu.VMEM(tile, F32),
            pltpu.VMEM(tile, F32),
            pltpu.VMEM(tile, F32),
            pltpu.VMEM(tile, F32),
            pltpu.VMEM((4, NZ), F32),
            pltpu.VMEM((4, NZ), I32),
            pltpu.VMEM((4, NX + 2, NYB, NZ), F32),
            pltpu.VMEM((4, NX + 2, NYB, NZ), F32),
            pltpu.VMEM((NX + 2, NYB, NZ), F32),
            pltpu.VMEM(brick, F32),
            pltpu.VMEM(brick, F32),
            pltpu.VMEM((2,) + rows, F32),
            pltpu.VMEM((2, 2, 4) + rows, F32),
            pltpu.VMEM((2, 4) + rows, F32),
            pltpu.VMEM((2, 4) + rows, F32),
            pltpu.VMEM((3,) + brick, F32),
            pltpu.VMEM(brick, F32),
            pltpu.VMEM((NX, OWNERS, NZ), BF16),
            pltpu.VMEM(rows, I32),
            pltpu.VMEM((N_SPAN, 2, LANES), I32),
            pltpu.VMEM((14, PR, NZ), F32),
            pltpu.VMEM((7, PR, NZ), F32),
            pltpu.VMEM((3, PR, NZ), F32),
            pltpu.VMEM((2, PR, NZ), F32),
            pltpu.VMEM((2, STRIP, 1, NZ), F32),
            pltpu.VMEM((2, STRIP, 1, NZ), F32),
            pltpu.VMEM((2, 8 * SLOTS, OWNERS), F32),
            pltpu.VMEM((OWNERS, 4, LANES), F32),
            pltpu.VMEM((N_SPAN, 4, LANES), F32),
            pltpu.VMEM((N_SPAN, 4, LANES), F32),
            pltpu.VMEM((N_SPAN, 2, LANES), I32),
            pltpu.VMEM((32, 2 * N_SPAN * LANES), BF16),
            pltpu.VMEM((LANES, 2 * N_SPAN * LANES), BF16),
            pltpu.VMEM((4, 8, LANES), I32),
            pltpu.VMEM((4, 8, LANES), F32),
            pltpu.VMEM((2, 8, LANES), F32),
            pltpu.VMEM((2, 8, LANES), F32),
            pltpu.VMEM((2 * N_SPAN, LANES), I32),
            pltpu.VMEM((N_SPAN, 2, LANES), F32),
            dma((10,)), dma((8,)), dma((4,)), dma((4,)), dma((4,)), dma((4,)), dma((2,)), dma((2,)),
            dma((6,)), dma((6,)),
        ],
        compiler_params=pltpu.CompilerParams(
            collective_id=0, has_side_effects=True, vmem_limit_bytes=40 * MB
        ),
        name="accretion",
    )(
        *map(
            hbm,
            (
                volume_fraction, droplet_momentum, air_velocity, drag,
                wall_owner.reshape(rows), wall_face,
                film.reshape(tile), ice.reshape(tile), cooling.reshape(tile), shed.reshape(tile),
                share, upstream,
            ),
        )
    )

    fraction_out, momentum_out, film_out, ice_out, displacement = pl.pallas_call(
        output_kernel,
        out_shape=(
            shape(brick), shape((3,) + brick), shape(tile), shape(tile), shape(brick),
        ),
        in_specs=[VM] * 6,
        out_specs=(HBM,) * 5,
        scratch_shapes=[
            pltpu.VMEM((8 * SLOTS, OWNERS), F32),
            pltpu.VMEM((8, LANES), F32),
            pltpu.VMEM(brick, F32),
            dma((8,)),
        ],
        compiler_params=pltpu.CompilerParams(vmem_limit_bytes=32 * MB),
        name="results",
    )(frac, mom, film_now, ice_now, ice_slots, keys)
    return fraction_out, momentum_out, film_out.reshape(-1), ice_out.reshape(-1), displacement


def solution(mesh):
    volume = P("span", "normal", None)
    vector = P(None, "span", "normal", None)
    faces = P(("span", "normal"))
    links = P(None, ("span", "normal"))
    return jax.shard_map(
        per_device,
        mesh=mesh,
        in_specs=(
            volume, vector, vector, volume, P("span", None, None), P("span", None),
            faces, faces, faces, faces, links, links,
        ),
        out_specs=(volume, vector, faces, faces, volume),
        check_vma=False,
    )
```

```python
import functools

import jax
import jax.numpy as jnp
from jax import lax
from jax.experimental import pallas as pl
from jax.experimental.pallas import tpu as pltpu
from jax.sharding import PartitionSpec as P

F32 = jnp.float32
BF16 = jnp.bfloat16
I32 = jnp.int32
MESH = pl.DeviceIdType.MESH
pseudo_step = 0.15
impact_rate = 4.0
half_step = 0.5 * pseudo_step
NX = 16
NYB = 16
NZ = 1024
LANES = 128
CH = NZ // LANES
N_SPAN = 16
N_NORMAL = 8
OWNERS = N_SPAN * N_NORMAL
SLOTS = 32
MB = 1 << 20
NT = (((1,), (1,)), ((), ()))


def iota(shape, dim):
    return lax.broadcasted_iota(I32, shape, dim)


def sweep_layer(S, V0, V1, V2, VN, NR, AIR, DRAG, emit):
    lane = iota((NYB, LANES), 1)
    row = iota((NYB, LANES), 0)
    last_lane, first_lane = lane == LANES - 1, lane == 0
    last_row, first_row = row == NYB - 1, row == 0

    def chord(c):
        zs = pl.ds(c * LANES, LANES)
        return [S(k, 0, zs) for k in range(4)] + [V2(zs)]

    here = chord(0)
    here_rolled = [pltpu.roll(t, LANES - 1, 1) for t in here]
    before = None
    for c in range(CH):
        zs = pl.ds(c * LANES, LANES)
        if c < CH - 1:
            after = chord(c + 1)
            after_rolled = [pltpu.roll(t, LANES - 1, 1) for t in after]
        else:
            after = after_rolled = [jnp.zeros((NYB, LANES), F32)] * 5
        f, v2 = here[:4], here[4]
        up = [jnp.where(last_lane, after_rolled[i], here_rolled[i]) for i in range(5)]
        w = v2 + up[4]
        pos = w > 0
        flux = [jnp.where(pos, f[k], up[k]) * w for k in range(4)]
        rolled = [pltpu.roll(t, 1, 1) for t in flux]
        if c == 0:
            edge = jnp.minimum(v2, 0.0)
            before = [edge * f[k] for k in range(4)]
        acc = [f[k] - (flux[k] - jnp.where(first_lane, before[k], rolled[k])) for k in range(4)]
        before = rolled

        v1 = V1(zs)
        w = v1 + jnp.where(last_row, VN(1, zs), pltpu.roll(v1, NYB - 1, 0))
        pos = w > 0
        w_low = VN(0, zs) + v1[0:1]
        pos_low = w_low > 0
        for k in range(4):
            upper = jnp.where(last_row, NR(1, k, zs), pltpu.roll(f[k], NYB - 1, 0))
            flux_k = jnp.where(pos, f[k], upper) * w
            low = jnp.where(pos_low, NR(0, k, zs), f[k][0:1]) * w_low
            acc[k] = acc[k] - (flux_k - jnp.where(first_row, low, pltpu.roll(flux_k, 1, 0)))

        v0 = V0(0, zs)
        w = v0 + V0(1, zs)
        w_low = V0(-1, zs) + v0
        pos, pos_low = w > 0, w_low > 0
        for k in range(4):
            flux_k = jnp.where(pos, f[k], S(k, 1, zs)) * w
            low = jnp.where(pos_low, S(k, -1, zs), f[k]) * w_low
            acc[k] = acc[k] - (flux_k - low)

        pull = pseudo_step * DRAG(zs)
        for k in range(3):
            acc[1 + k] = acc[1 + k] + pull * (f[0] * AIR(k, zs) - f[1 + k])
        emit(c, zs, acc, v0, v1, v2)
        here, here_rolled = after, after_rolled


def advance(S, V0, V1, V2, VN, NR, AIR, DRAG, emit, x):
    sweep_layer(
        lambda k, d, zs: S[k, x + d, :, zs],
        lambda d, zs: V0[x + d, :, zs],
        lambda zs: V1[x - 1, :, zs],
        lambda zs: V2[x - 1, :, zs],
        lambda side, zs: VN[side, x - 1, :, zs],
        lambda side, k, zs: NR[side, k, x - 1, :, zs],
        lambda k, zs: AIR[k, x - 1, :, zs],
        lambda zs: DRAG[x - 1, :, zs],
        emit,
    )


def prepare(owner_ref, face_ref, rank_ref, key8_ref, send_ref, hot_ref, n, h):
    q_len = 256
    quarters = NZ // q_len
    tri = (iota((q_len, q_len), 0) <= iota((q_len, q_len), 1)).astype(F32).astype(BF16)
    names = iota((OWNERS, q_len), 0)
    mine = N_NORMAL * iota((N_SPAN, NZ), 0) + n
    slot = iota((SLOTS, NZ), 0)
    pieces = []
    for b in range(4):
        offset = jnp.zeros((OWNERS, 1), F32)
        got = jnp.zeros((N_SPAN, 2 * SLOTS), F32)
        for half in range(2):
            x = h * 8 + b * 2 + half
            owner = owner_ref[x]
            hots = []
            for q in range(quarters):
                qs = slice(q * q_len, (q + 1) * q_len)
                hot = (owner[:, qs] == names).astype(F32).astype(BF16)
                hot_ref[x, :, qs] = hot
                hots.append(hot)
            counts = jnp.dot(
                jnp.concatenate(hots, axis=0), tri, preferred_element_type=F32
            )
            ranks = []
            for q in range(quarters):
                part = counts[q * OWNERS : (q + 1) * OWNERS]
                ranks.append(
                    jnp.sum(hots[q].astype(F32) * (part + offset), axis=0, keepdims=True) - 1.0
                )
                offset = offset + part[:, q_len - 1 : q_len]
            rank = jnp.concatenate(ranks, axis=1).astype(I32)
            rank_ref[x] = rank
            key = owner * SLOTS + rank
            for t in range(CH):
                key8_ref[x, t : t + 1, :] = key[:, t * LANES : (t + 1) * LANES]
            face = face_ref[x : x + 1, :]
            at = slot == rank
            high = jnp.where(at, (face >> 7).astype(F32), 0.0)
            low = jnp.where(at, (face & 127).astype(F32), 0.0)
            placed = jnp.concatenate([high, low], axis=0).astype(BF16)
            hot16 = (owner == mine).astype(F32).astype(BF16)
            got = got + lax.dot_general(hot16, placed, NT, preferred_element_type=F32)
        pieces.append(got[:, :SLOTS] * 128.0 + got[:, SLOTS:])
    send_ref[:, h, :] = jnp.concatenate(pieces, axis=1).astype(I32)


PR = 24
FR = (0, 1, 2)
MS = (3, 4)
MN = (5, 6, 7)
MC = (8, 9)
AN = (10, 11)
DR = (12, 13)
NEAR = (0, 1, 3, 4, 5, 6, 8, 10, 12)
FAR = (0, 3, 5)
STRIP = len(NEAR) + len(FAR)


def flux_of(w, low, high):
    return jnp.where(w > 0, low, high) * w


def wall_strip(pk, vq, q1, wv):
    lane = iota((PR, LANES), 1)
    last_lane, first_lane = lane == LANES - 1, lane == 0

    def tile(ref, i, t):
        return ref[i, :, t * LANES : (t + 1) * LANES]

    def next_tile(ref, i, t):
        here = pltpu.roll(tile(ref, i, t), LANES - 1, 1)
        if t == CH - 1:
            return jnp.where(last_lane, 0.0, here)
        return jnp.where(last_lane, pltpu.roll(tile(ref, i, t + 1), LANES - 1, 1), here)

    def spanwise(f, v):
        flux = flux_of(v + pltpu.roll(v, PR - 1, 0), f, pltpu.roll(f, PR - 1, 0))
        return flux - pltpu.roll(flux, 1, 0)

    def chordwise(ref, i, f, v, v_next, t, before):
        flux = flux_of(v + v_next, f, next_tile(ref, i, t))
        rolled = pltpu.roll(flux, 1, 1)
        if t == 0:
            before = jnp.minimum(v, 0.0) * f
        return flux - jnp.where(first_lane, before, rolled), rolled

    for y in range(3):
        for t in range(CH):
            zs = slice(t * LANES, (t + 1) * LANES)
            scale = half_step / tile(pk, FR[y], t)
            vq[2 + y, :, zs] = tile(pk, MN[y], t) * scale
            if y < 2:
                vq[y, :, zs] = tile(pk, MS[y], t) * scale
                vq[5 + y, :, zs] = tile(pk, MC[y], t) * scale

    before = [None] * 3
    for t in range(CH):
        zs = slice(t * LANES, (t + 1) * LANES)
        v0, v0_1 = tile(vq, 0, t), tile(vq, 1, t)
        v1, v1_1, v1_2 = tile(vq, 2, t), tile(vq, 3, t), tile(vq, 4, t)
        v2, v2_1 = tile(vq, 5, t), tile(vq, 6, t)
        v2_next, v2_1_next = next_tile(vq, 5, t), next_tile(vq, 6, t)
        a0, a1 = tile(pk, FR[0], t), tile(pk, FR[1], t)
        m0, m1, m2 = (tile(pk, i, t) for i in MN)
        w0, w1 = v1 + v1_1, v1_1 + v1_2
        wall = jnp.minimum(v1, 0.0)
        along, before[0] = chordwise(pk, FR[0], a0, v2, v2_next, t, before[0])
        q1[0, :, zs] = (
            a0 - along - spanwise(a0, v0) - (flux_of(w0, a0, a1) - wall * a0)
        )
        between = flux_of(w0, m0, m1)
        along, before[1] = chordwise(pk, MN[0], m0, v2, v2_next, t, before[1])
        q1[1, :, zs] = (
            m0 - along - spanwise(m0, v0) - (between - wall * m0)
            + pseudo_step * tile(pk, DR[0], t) * (a0 * tile(pk, AN[0], t) - m0)
        )
        along, before[2] = chordwise(pk, MN[1], m1, v2_1, v2_1_next, t, before[2])
        q1[2, :, zs] = (
            m1 - along - spanwise(m1, v0_1) - (flux_of(w1, m1, m2) - between)
            + pseudo_step * tile(pk, DR[1], t) * (a1 * tile(pk, AN[1], t) - m1)
        )

    before = None
    for t in range(CH):
        zs = slice(t * LANES, (t + 1) * LANES)
        v0, v1, v1_1, v2 = (tile(vq, i, t) for i in (0, 2, 3, 5))
        a0, m0, m1 = (tile(q1, i, t) for i in range(3))
        along, before = chordwise(q1, 1, m0, v2, next_tile(vq, 5, t), t, before)
        out = (
            m0 - along - spanwise(m0, v0)
            - (flux_of(v1 + v1_1, m0, m1) - jnp.minimum(v1, 0.0) * m0)
            + pseudo_step * tile(pk, DR[0], t) * (a0 * tile(pk, AN[0], t) - m0)
        )
        catch = jnp.maximum(-out, 0.0)
        wv[0, :, zs] = catch
        wv[1, :, zs] = (
            catch * (0.5 / (half_step * half_step)) * (v0 * v0 + v1 * v1 + v2 * v2)
        )


def main_kernel(
    a_hbm, m_hbm, air_hbm, drag_hbm, owner_hbm, face_hbm,
    film_hbm, ice_hbm, cool_hbm, shed_hbm, share_hbm, up_hbm,
    frac_out, mom_out, film_out, ice_out, all_ref, key8_ref,
    owner_ref, face_ref, film_ref, ice_ref, cool_ref, shed_ref, share_ref, up_ref,
    s_ref, s1_ref, v0_ref, v1_ref, v2_ref, vn_ref, ns_ref, nr_ref, nr2_ref, air_ref, drag_ref,
    owner_hot, rank_ref, sendface_ref, pk, vq, q1, wv, strip_out, strip_in,
    slots_ref, fw_ref, got_ref, gotface_ref, prevface_ref, lhs_ref, hot_ref, gone_ref,
    links_ref, weight_ref, prev_ref, out_ref, pack_ref, prevpack_ref, back_ref, col_ref,
    load_sem, small_sem, span_send, span_recv, normal_send, normal_recv, strip_send, strip_recv, sends, recvs, ready,
):
    c, n = lax.axis_index("span"), lax.axis_index("normal")
    right, left = (c + 1) % N_SPAN, (c + N_SPAN - 1) % N_SPAN
    on_wall, has_low, has_high = n == 0, n > 0, n < N_NORMAL - 1
    off_wall = has_low
    last_of_column = n == N_NORMAL - 1
    has_next = jnp.logical_or(has_high, c < N_SPAN - 1)
    has_prev = jnp.logical_or(has_low, c > 0)
    next_c, next_n = jnp.where(last_of_column, c + 1, c), jnp.where(last_of_column, 0, n + 1)
    prev_c, prev_n = jnp.where(on_wall, c - 1, c), jnp.where(on_wall, N_NORMAL - 1, n - 1)
    cross_next = jnp.logical_and(last_of_column, c < N_SPAN - 1)
    cross_prev = jnp.logical_and(on_wall, c > 0)

    first_loads = [
        pltpu.make_async_copy(src, dst, small_sem.at[i])
        for i, (src, dst) in enumerate(((owner_hbm, owner_ref), (face_hbm, face_ref)))
    ]
    low, high = pl.ds(0, 8), pl.ds(8, 8)
    whole = pl.ds(1, NX)
    low_loads = [
        pltpu.make_async_copy(src, dst, load_sem.at[i])
        for i, (src, dst) in enumerate(
            (
                (a_hbm.at[:, low], s_ref.at[0, whole, low]),
                (m_hbm.at[:, :, low], s_ref.at[pl.ds(1, 3), whole, low]),
                (air_hbm.at[1, :, low], air_ref.at[1, :, low]),
                (drag_hbm.at[:, low], drag_ref.at[:, low]),
            )
        )
    ]
    loads = [
        pltpu.make_async_copy(src, dst, load_sem.at[4 + i])
        for i, (src, dst) in enumerate(
            (
                (a_hbm.at[:, high], s_ref.at[0, whole, high]),
                (m_hbm.at[:, :, high], s_ref.at[pl.ds(1, 3), whole, high]),
                (air_hbm.at[1, :, high], air_ref.at[1, :, high]),
                (drag_hbm.at[:, high], drag_ref.at[:, high]),
                (air_hbm.at[0], air_ref.at[0]),
                (air_hbm.at[2], air_ref.at[2]),
            )
        )
    ] + [
        pltpu.make_async_copy(src, dst, small_sem.at[2 + i])
        for i, (src, dst) in enumerate(
            ((film_hbm, film_ref), (ice_hbm, ice_ref), (cool_hbm, cool_ref), (shed_hbm, shed_ref),
             (share_hbm, share_ref), (up_hbm, up_ref))
        )
    ]
    for load in first_loads + low_loads + loads:
        load.start()

    barrier = pltpu.get_barrier_semaphore()

    @pl.loop(1, N_SPAN)
    def _(i):
        pl.semaphore_signal(barrier, 1, device_id=((c + i) % N_SPAN, n), device_id_type=MESH)

    @pl.loop(1, N_NORMAL)
    def _(i):
        pl.semaphore_signal(barrier, 1, device_id=(c, (n + i) % N_NORMAL), device_id_type=MESH)

    @pl.when(cross_next)
    def _():
        pl.semaphore_signal(barrier, 1, device_id=(next_c, next_n), device_id_type=MESH)

    @pl.when(cross_prev)
    def _():
        pl.semaphore_signal(barrier, 1, device_id=(prev_c, prev_n), device_id_type=MESH)

    for load in first_loads:
        load.wait()
    prepare(owner_ref, face_ref, rank_ref, key8_ref, sendface_ref, owner_hot, n, 0)
    for load in low_loads:
        load.wait()

    def packed_row(i, x):
        if i in FR:
            return s_ref[0, x + 1, FR.index(i) : FR.index(i) + 1, :]
        for k, sets in ((1, MS), (2, MN), (3, MC)):
            if i in sets:
                y = sets.index(i)
                return s_ref[k, x + 1, y : y + 1, :]
        if i in AN:
            return air_ref[1, x, AN.index(i) : AN.index(i) + 1, :]
        return drag_ref[x, DR.index(i) : DR.index(i) + 1, :]

    @pl.when(on_wall)
    def _():
        for side, near, far in ((0, NX - 1, NX - 2), (1, 0, 1)):
            for j, i in enumerate(NEAR):
                strip_out[side, j] = packed_row(i, near)
            for j, i in enumerate(FAR):
                strip_out[side, len(NEAR) + j] = packed_row(i, far)

    @pl.when(jnp.logical_not(has_prev))
    def _():
        prev_ref[...] = jnp.zeros((8, LANES), F32)
        prevpack_ref[...] = jnp.ones((4, 8, LANES), F32)
        prevface_ref[...] = jnp.zeros((N_SPAN, 2, LANES), I32)

    crossing = jnp.logical_or(cross_next, cross_prev)
    peers = N_SPAN + N_NORMAL - 2

    @pl.when(crossing)
    def _():
        pl.semaphore_wait(barrier, peers + 1)

    @pl.when(jnp.logical_not(crossing))
    def _():
        pl.semaphore_wait(barrier, peers)

    def remote(src, dst, send, recv, device):
        return pltpu.make_async_remote_copy(
            src_ref=src, dst_ref=dst, send_sem=send, recv_sem=recv,
            device_id=device, device_id_type=MESH,
        )

    def await_bytes(ref, sem):
        pltpu.make_async_copy(ref, ref, sem).wait()

    def far_first(place, i):
        return (place + jnp.where(i == 3, 0, jnp.where(i == 0, 2, 2 * i - 1))) & 3

    def row_peer(i):
        return far_first(c >> 2, i >> 2) * 4 + far_first(c & 3, i & 3)

    sides = [2 * ((n >> 1) + j & 3) + core for j in (2, 1, 3, 0) for core in range(2)]
    here_last = [2 * ((n >> 1) + j & 3) + core for j in (2, 1, 3) for core in range(2)] + [n ^ 1]

    def to_all(src, dst, which):
        @pl.loop(0, N_SPAN - 1)
        def _(i):
            there = row_peer(i)
            for side in sides:
                remote(src(there, side), dst, sends.at[which], recvs.at[which],
                       (there, side)).start()

        for side in here_last:
            remote(src(c, side), dst, sends.at[which], recvs.at[which], (c, side)).start()

    def to_row(src, dst, which):
        @pl.loop(0, N_SPAN - 1)
        def _(i):
            there = row_peer(i)
            remote(src.at[there], dst.at[c], sends.at[which], recvs.at[which], (there, n)).start()

    strips = [
        remote(
            strip_out.at[side], strip_in.at[side], strip_send.at[side], strip_recv.at[side],
            (there, n),
        )
        for side, there in ((0, right), (1, left))
    ]

    @pl.when(on_wall)
    def _():
        for copy in strips:
            copy.start()

        @pl.loop(1, N_SPAN)
        def _(i):
            pl.semaphore_signal(ready, 1, device_id=((c + i) % N_SPAN, n), device_id_type=MESH)

    def normal_copies(base, dst, sem, start, size):
        part = pl.ds(start, size)
        return (
            remote(ns_ref.at[base, 0, :, part], dst.at[1, :, part], normal_send.at[2 * sem],
                   normal_recv.at[2 * sem], (c, n - 1)),
            remote(ns_ref.at[base, 1, :, part], dst.at[0, :, part], normal_send.at[2 * sem + 1],
                   normal_recv.at[2 * sem + 1], (c, n + 1)),
        )

    def start_normal(*which):
        low, high = normal_copies(*which)

        @pl.when(has_low)
        def _():
            low.start()

        @pl.when(has_high)
        def _():
            high.start()

    def wait_normal(*which):
        low, high = normal_copies(*which)

        @pl.when(has_low)
        def _():
            low.wait_send()
            high.wait_recv()

        @pl.when(has_high)
        def _():
            high.wait_send()
            low.wait_recv()

    def close_edges(dst):
        @pl.when(jnp.logical_not(has_low))
        def _():
            dst[0] = jnp.zeros(dst.shape[1:], F32)

        @pl.when(jnp.logical_not(has_high))
        def _():
            dst[1] = jnp.zeros(dst.shape[1:], F32)

    def span_copies(src, dst, base):
        return [
            remote(src.at[:, layer], dst.at[:, target], span_send.at[base + i],
                   span_recv.at[base + i], (there, n))
            for i, (there, layer, target) in enumerate(((right, NX, 0), (left, 1, NX + 1)))
        ]

    for load in loads:
        load.wait()

    @pl.loop(0, NX)
    def _(x):
        for k in range(4):
            ns_ref[0, 0, k, x] = s_ref[k, x + 1, 0:1, :]
            ns_ref[0, 1, k, x] = s_ref[k, x + 1, NYB - 1 : NYB, :]

    first_halo = (0, nr_ref, 0, 0, NX)
    again_halo = [
        (1, nr2_ref, 1 + i, start, size) for i, (start, size) in enumerate(((1, 8), (9, 7), (0, 1)))
    ]
    start_normal(*first_halo)
    close_edges(nr_ref)
    close_edges(nr2_ref)
    spans = span_copies(s_ref, s_ref, 0)
    for copy in spans:
        copy.start()
    film0 = film_ref[...]
    shed = shed_ref[...]
    outflow0 = film0 * shed
    out_ref[...] = outflow0

    def pass_on(src, dst, which):
        return remote(src, dst, sends.at[which], recvs.at[which], (next_c, next_n))

    @pl.when(has_next)
    def _():
        pass_on(out_ref, prev_ref, 1).start()

    prepare(owner_ref, face_ref, rank_ref, key8_ref, sendface_ref, owner_hot, n, 1)
    to_row(sendface_ref, gotface_ref, 0)
    gotface_ref[c] = sendface_ref[c]

    @pl.loop(0, NX)
    def _(x):
        scale = half_step / s_ref[0, x + 1]
        v0_ref[x + 1] = s_ref[1, x + 1] * scale
        v1_ref[x] = s_ref[2, x + 1] * scale
        v2_ref[x] = s_ref[3, x + 1] * scale

    @pl.when(on_wall)
    def _():
        for i in range(14):
            pk[i, 0:8, :] = jnp.ones((8, NZ), F32)
            pk[i, 16:24, :] = jnp.ones((8, NZ), F32)
        for x in range(NX):
            for i in range(14):
                pk[i, x + 2 : x + 3, :] = packed_row(i, x)
        for copy in strips:
            copy.wait()
        for side, near, far in ((0, 1, 0), (1, NX + 2, NX + 3)):
            for j, i in enumerate(NEAR):
                pk[i, near : near + 1, :] = strip_in[side, j]
            for j, i in enumerate(FAR):
                pk[i, far : far + 1, :] = strip_in[side, len(NEAR) + j]
        wall_strip(pk, vq, q1, wv)
        slot = iota((SLOTS, NZ), 0)

        @pl.loop(0, NX // 2, unroll=2)
        def _(b):
            total = jnp.zeros((4 * SLOTS, OWNERS), F32)
            for half in range(2):
                x = b * 2 + half
                at = slot == rank_ref[x]
                rows = []
                for split in range(2):
                    for v in range(2):
                        value = wv[v, pl.ds(x + 2, 1), :]
                        high = value.astype(BF16).astype(F32)
                        rows.append(jnp.where(at, high if split == 0 else value - high, 0.0))
                weights = jnp.concatenate(rows, axis=0).astype(BF16)
                total = total + lax.dot_general(
                    weights, owner_hot[x], NT, preferred_element_type=F32
                )
            both = total[: 2 * SLOTS] + total[2 * SLOTS :]
            spot = pl.ds(pl.multiple_of(b * SLOTS, SLOTS), SLOTS)
            slots_ref[0, spot, :] = both[:SLOTS]
            slots_ref[1, spot, :] = both[SLOTS:]

        fw_ref[0] = jnp.zeros((4, LANES), F32)
        for v in range(2):
            for h in range(2):
                fw_ref[1:, 2 * v + h, :] = slots_ref[v, h * LANES : (h + 1) * LANES, :].T
        pl.semaphore_wait(ready, N_SPAN - 1)

        to_all(
            lambda there, side: fw_ref.at[pl.ds(there * N_NORMAL + side, 2)], got_ref.at[c], 3
        )
        got_ref[c] = fw_ref[pl.ds(c * N_NORMAL, 2)]

    for k in range(4):
        for t in range(8):
            links_ref[k, t : t + 1, :] = up_ref[k : k + 1, t * LANES : (t + 1) * LANES]
            weight_ref[k, t : t + 1, :] = share_ref[k : k + 1, t * LANES : (t + 1) * LANES]
    await_bytes(gotface_ref.at[pl.ds(0, N_SPAN - 1)], recvs.at[0])
    lanes_high = iota((LANES, LANES), 0)

    @pl.when(has_next)
    def _():
        pass_on(gotface_ref, prevface_ref, 4).start()

    def face_tables(faces_ref, which):
        for s in range(2 * N_SPAN):
            face = faces_ref[s // 2][s % 2 : s % 2 + 1]
            hot_ref[which, :, s * LANES : (s + 1) * LANES] = (
                (lanes_high == (face & 127)).astype(F32).astype(BF16)
            )
            back_ref[which, s : s + 1, :] = face

    face_tables(gotface_ref, 1)

    @pl.when(has_prev)
    def _():
        await_bytes(prev_ref, recvs.at[1])

    first_face = (c * N_NORMAL + n) * 1024

    def runin(before, own):
        total = jnp.zeros((8, LANES), F32)
        for k in range(4):
            link = links_ref[k]
            spot = link - (first_face - 1024)
            low, high = spot & 127, spot >> 7
            picked = jnp.zeros((8, LANES), F32)
            for j in range(16):
                line = before[j : j + 1] if j < 8 else own[j - 8 : j - 7]
                value = jnp.take_along_axis(
                    jnp.broadcast_to(line, (8, LANES)), low, axis=1, mode="promise_in_bounds"
                )
                picked = jnp.where(high == j, value, picked)
            total = total + weight_ref[k] * jnp.where(link >= 0, picked, 0.0)
        return total

    run0 = runin(prev_ref[...], outflow0)
    for i, value in enumerate((film0, shed, cool_ref[...], run0)):
        pack_ref[i] = value

    @pl.when(has_next)
    def _():
        pass_on(pack_ref, prevpack_ref, 2).start()

    wait_normal(*first_halo)

    def edge_speed(side, present):
        @pl.when(present)
        def _():
            @pl.loop(0, NX)
            def _(x):
                vn_ref[side, x] = nr_ref[side, 2, x] * (half_step / nr_ref[side, 0, x])

        @pl.when(jnp.logical_not(present))
        def _():
            vn_ref[side] = jnp.zeros(vn_ref.shape[1:], F32)

    edge_speed(0, has_low)
    edge_speed(1, has_high)

    again = span_copies(s1_ref, s1_ref, 2)

    @pl.loop(0, NX)
    def _(i):
        @pl.when(i == 8)
        def _():
            start_normal(*again_halo[0])
            for copy in spans:
                copy.wait()
            for edge in (0, NX + 1):
                v0_ref[edge] = s_ref[1, edge] * (half_step / s_ref[0, edge])

        @pl.when(i == 10)
        def _():
            for copy in again:
                copy.start()

        x = jnp.where(i < 8, i + 2, jnp.where(i == 8, 1, jnp.where(i == 9, NX, i)))

        def emit(t, zs, acc, v0, v1, v2):
            for k in range(4):
                s1_ref[k, x, :, zs] = acc[k]
                ns_ref[1, 0, k, x - 1, :, zs] = acc[k][0:1]
                ns_ref[1, 1, k, x - 1, :, zs] = acc[k][NYB - 1 : NYB]

        advance(s_ref, v0_ref, v1_ref, v2_ref, vn_ref, nr_ref, air_ref, drag_ref, emit, x)

    start_normal(*again_halo[1])
    start_normal(*again_halo[2])

    @pl.when(has_prev)
    def _():
        await_bytes(prevface_ref, recvs.at[4])
        await_bytes(prevpack_ref, recvs.at[2])

    face_tables(prevface_ref, 0)

    @pl.when(on_wall)
    def _():
        await_bytes(got_ref.at[pl.ds(0, N_SPAN - 1)], recvs.at[3])

    @pl.when(off_wall)
    def _():
        await_bytes(got_ref, recvs.at[3])

    eight = iota((8, LANES), 0)

    def face_sums(which):
        for s in range(2 * N_SPAN):
            at = eight == (back_ref[which, s : s + 1, :] >> 7)
            values = [
                got_ref[s // 2, which, 2 * v + s % 2 : 2 * v + s % 2 + 1, :] for v in range(2)
            ]
            highs = [value.astype(BF16).astype(F32) for value in values]
            rows = []
            for part in (highs, [values[v] - highs[v] for v in range(2)]):
                rows.extend(jnp.where(at, part[v], 0.0) for v in range(2))
            lhs_ref[which, :, s * LANES : (s + 1) * LANES] = (
                jnp.concatenate(rows, axis=0).astype(BF16)
            )
        sums = lax.dot_general(
            lhs_ref[which], hot_ref[which], NT, preferred_element_type=F32
        )
        sums = sums[:16] + sums[16:]
        return sums[:8], sums[8:]

    def film_step(film, outflow, run, catch, heat):
        inflow = impact_rate * catch + film - outflow + run
        frozen = heat * inflow / (heat + inflow)
        return inflow - frozen, frozen

    prev_catch, prev_kinetic = face_sums(0)
    face_catch, face_kinetic = face_sums(1)
    heat = cool_ref[...] / (1.0 + face_kinetic)
    prev_film, prev_shed, prev_cool, prev_run = (prevpack_ref[i] for i in range(4))
    prev_film1, _ = film_step(
        prev_film, prev_ref[...], prev_run, prev_catch, prev_cool / (1.0 + prev_kinetic)
    )
    film1, frozen1 = film_step(film0, outflow0, run0, face_catch, heat)
    outflow1 = film1 * shed
    run1 = runin(prev_film1 * prev_shed, outflow1)
    film2, frozen2 = film_step(film1, outflow1, run1, face_catch, heat)
    film_out[...] = film2
    ice2 = ice_ref[...] + frozen1 + frozen2
    ice_out[...] = ice2

    for g in range(4):
        faces = back_ref[1, g * 8 : g * 8 + 8, :]
        low, high = faces & 127, faces >> 7
        picked = jnp.zeros((8, LANES), F32)
        for j in range(8):
            value = jnp.take_along_axis(
                jnp.broadcast_to(ice2[j : j + 1], (8, LANES)), low, axis=1,
                mode="promise_in_bounds",
            )
            picked = jnp.where(high == j, value, picked)
        for i in range(4):
            col_ref[g * 4 + i] = picked[2 * i : 2 * i + 2]
    to_all(lambda there, side: col_ref.at[there], all_ref.at[c * N_NORMAL + n], 5)
    all_ref[c * N_NORMAL + n] = col_ref[c]


    @pl.loop(0, NX)
    def _(i):
        for at, part in ((0, 0), (8, 1), (NX - 2, 2)):
            @pl.when(i == at)
            def _():
                wait_normal(*again_halo[part])

        @pl.when(i == NX - 2)
        def _():
            for copy in again:
                copy.wait()

        x = jnp.where(i < NX - 2, i + 2, jnp.where(i == NX - 2, 1, NX))

        def emit(t, zs, acc, v0, v1, v2):
            frac_out[x - 1, :, zs] = acc[0]
            for k in range(3):
                mom_out[k, x - 1, :, zs] = acc[1 + k]

        advance(s1_ref, v0_ref, v1_ref, v2_ref, vn_ref, nr2_ref, air_ref, drag_ref, emit, x)

    await_bytes(all_ref.at[pl.ds(0, OWNERS - 1)], recvs.at[5])

    await_bytes(sendface_ref.at[pl.ds(0, N_SPAN - 1)], sends.at[0])

    @pl.when(has_next)
    def _():
        await_bytes(out_ref, sends.at[1])
        await_bytes(pack_ref, sends.at[2])
        await_bytes(gotface_ref, sends.at[4])

    @pl.when(on_wall)
    def _():
        await_bytes(gone_ref, sends.at[3])

    await_bytes(all_ref.at[pl.ds(0, OWNERS - 1)], sends.at[5])


def output_kernel(
    frac_ref, mom_ref, film_ref, ice_ref, all_ref, key8_ref,
    frac_out, mom_out, film_out, ice_out, disp_out,
    pick_ref, row_ref, disp_ref, sems,
):
    n = lax.axis_index("normal")
    put_m = pltpu.make_async_copy(mom_ref, mom_out, sems.at[0])
    put_a = pltpu.make_async_copy(frac_ref, frac_out, sems.at[1])
    put_m.start()
    put_a.start()
    put_film = pltpu.make_async_copy(film_ref, film_out, sems.at[6])
    put_ice = pltpu.make_async_copy(ice_ref, ice_out, sems.at[7])
    put_film.start()
    put_ice.start()

    for h in range(2):
        pick_ref[h * LANES : (h + 1) * LANES, :] = (
            all_ref[:, h, :].T
        )
    y = (n * NYB + iota((NYB, LANES), 0)).astype(F32) + 0.5
    left = 1.0 - y / (NYB * N_NORMAL)
    profile = left * left
    group = 4
    puts = []
    for g in range(NX // group):

        @pl.loop(g * group, (g + 1) * group)
        def _(x):
            key = key8_ref[x]
            owner, rank = key >> 5, key & (SLOTS - 1)
            base = pl.multiple_of((x // 2) * SLOTS, SLOTS)
            table = pick_ref[pl.ds(base, SLOTS), :]
            picked = jnp.zeros((8, LANES), F32)
            for j in range(SLOTS):
                value = jnp.take_along_axis(
                    jnp.broadcast_to(table[j : j + 1], (8, LANES)), owner, axis=1,
                    mode="promise_in_bounds",
                )
                picked = jnp.where(rank == j, value, picked)
            row_ref[...] = picked
            for t in range(CH):
                disp_ref[x, :, t * LANES : (t + 1) * LANES] = row_ref[t : t + 1, :] * profile

        part = pl.ds(g * group, group)
        put = pltpu.make_async_copy(disp_ref.at[part], disp_out.at[part], sems.at[2 + g])
        put.start()
        puts.append(put)
    for put in (put_m, put_a, put_film, put_ice):
        put.wait()
    for put in puts:
        put.wait()


def shape(dims, dtype=F32):
    return jax.ShapeDtypeStruct(dims, dtype)


VM = pl.BlockSpec(memory_space=pltpu.VMEM)
HBM = pl.BlockSpec(memory_space=pltpu.HBM)


def per_device(
    volume_fraction, droplet_momentum, air_velocity, drag, wall_owner, wall_face,
    film, ice, cooling, shed, share, upstream,
):
    brick = (NX, NYB, NZ)
    tile = (8, LANES)
    rows = (NX, 1, NZ)
    hbm = functools.partial(pltpu.with_memory_space_constraint, memory_space=pltpu.HBM)
    dma = pltpu.SemaphoreType.DMA
    frac, mom, film_now, ice_now, ice_slots, keys = pl.pallas_call(
        main_kernel,
        out_shape=(
            shape(brick), shape((3,) + brick), shape(tile), shape(tile),
            shape((OWNERS, 2, LANES)), shape((NX, 8, LANES), I32),
        ),
        in_specs=[HBM] * 12,
        out_specs=(VM,) * 6,
        scratch_shapes=[
            pltpu.VMEM(rows, I32),
            pltpu.VMEM((NX, NZ), I32),
            pltpu.VMEM(tile, F32),
            pltpu.VMEM(tile, F32),
            pltpu.VMEM(tile, F32),
            pltpu.VMEM(tile, F32),
            pltpu.VMEM((4, NZ), F32),
            pltpu.VMEM((4, NZ), I32),
            pltpu.VMEM((4, NX + 2, NYB, NZ), F32),
            pltpu.VMEM((4, NX + 2, NYB, NZ), F32),
            pltpu.VMEM((NX + 2, NYB, NZ), F32),
            pltpu.VMEM(brick, F32),
            pltpu.VMEM(brick, F32),
            pltpu.VMEM((2,) + rows, F32),
            pltpu.VMEM((2, 2, 4) + rows, F32),
            pltpu.VMEM((2, 4) + rows, F32),
            pltpu.VMEM((2, 4) + rows, F32),
            pltpu.VMEM((3,) + brick, F32),
            pltpu.VMEM(brick, F32),
            pltpu.VMEM((NX, OWNERS, NZ), BF16),
            pltpu.VMEM(rows, I32),
            pltpu.VMEM((N_SPAN, 2, LANES), I32),
            pltpu.VMEM((14, PR, NZ), F32),
            pltpu.VMEM((7, PR, NZ), F32),
            pltpu.VMEM((3, PR, NZ), F32),
            pltpu.VMEM((2, PR, NZ), F32),
            pltpu.VMEM((2, STRIP, 1, NZ), F32),
            pltpu.VMEM((2, STRIP, 1, NZ), F32),
            pltpu.VMEM((2, 8 * SLOTS, OWNERS), F32),
            pltpu.VMEM((OWNERS + 1, 4, LANES), F32),
            pltpu.VMEM((N_SPAN, 2, 4, LANES), F32),
            pltpu.VMEM((N_SPAN, 2, LANES), I32),
            pltpu.VMEM((N_SPAN, 2, LANES), I32),
            pltpu.VMEM((2, 32, 2 * N_SPAN * LANES), BF16),
            pltpu.VMEM((2, LANES, 2 * N_SPAN * LANES), BF16),
            pltpu.VMEM((OWNERS - 1, 8, LANES), F32),
            pltpu.VMEM((4, 8, LANES), I32),
            pltpu.VMEM((4, 8, LANES), F32),
            pltpu.VMEM((8, LANES), F32),
            pltpu.VMEM((8, LANES), F32),
            pltpu.VMEM((4, 8, LANES), F32),
            pltpu.VMEM((4, 8, LANES), F32),
            pltpu.VMEM((2, 2 * N_SPAN, LANES), I32),
            pltpu.VMEM((N_SPAN, 2, LANES), F32),
            dma((10,)), dma((8,)), dma((4,)), dma((4,)), dma((8,)), dma((8,)), dma((2,)), dma((2,)),
            dma((6,)), dma((6,)), pltpu.SemaphoreType.REGULAR,
        ],
        compiler_params=pltpu.CompilerParams(
            collective_id=0, has_side_effects=True, vmem_limit_bytes=40 * MB
        ),
        name="accretion",
    )(
        *map(
            hbm,
            (
                volume_fraction, droplet_momentum, air_velocity, drag,
                wall_owner.reshape(rows), wall_face,
                film.reshape(tile), ice.reshape(tile), cooling.reshape(tile), shed.reshape(tile),
                share, upstream,
            ),
        )
    )

    fraction_out, momentum_out, film_out, ice_out, displacement = pl.pallas_call(
        output_kernel,
        out_shape=(
            shape(brick), shape((3,) + brick), shape(tile), shape(tile), shape(brick),
        ),
        in_specs=[VM] * 6,
        out_specs=(HBM,) * 5,
        scratch_shapes=[
            pltpu.VMEM((8 * SLOTS, OWNERS), F32),
            pltpu.VMEM((8, LANES), F32),
            pltpu.VMEM(brick, F32),
            dma((8,)),
        ],
        compiler_params=pltpu.CompilerParams(vmem_limit_bytes=32 * MB),
        name="results",
    )(frac, mom, film_now, ice_now, ice_slots, keys)
    return fraction_out, momentum_out, film_out.reshape(-1), ice_out.reshape(-1), displacement


def solution(mesh):
    volume = P("span", "normal", None)
    vector = P(None, "span", "normal", None)
    faces = P(("span", "normal"))
    links = P(None, ("span", "normal"))
    return jax.shard_map(
        per_device,
        mesh=mesh,
        in_specs=(
            volume, vector, vector, volume, P("span", None, None), P("span", None),
            faces, faces, faces, faces, links, links,
        ),
        out_specs=(volume, vector, faces, faces, volume),
        check_vma=False,
    )
```

```python
import functools

import jax
import jax.numpy as jnp
from jax import lax
from jax.experimental import pallas as pl
from jax.experimental.pallas import tpu as pltpu
from jax.sharding import PartitionSpec as P

F32 = jnp.float32
BF16 = jnp.bfloat16
I32 = jnp.int32
MESH = pl.DeviceIdType.MESH
pseudo_step = 0.15
impact_rate = 4.0
half_step = 0.5 * pseudo_step
NX = 16
NYB = 16
NZ = 1024
LANES = 128
CH = NZ // LANES
N_SPAN = 16
N_NORMAL = 8
OWNERS = N_SPAN * N_NORMAL
SLOTS = 32
MB = 1 << 20
NT = (((1,), (1,)), ((), ()))


def iota(shape, dim):
    return lax.broadcasted_iota(I32, shape, dim)


def sweep_layer(S, V0, V1, V2, VN, NR, AIR, DRAG, emit):
    lane = iota((NYB, LANES), 1)
    row = iota((NYB, LANES), 0)
    last_lane, first_lane = lane == LANES - 1, lane == 0
    last_row, first_row = row == NYB - 1, row == 0

    def chord(c):
        zs = pl.ds(c * LANES, LANES)
        return [S(k, 0, zs) for k in range(4)] + [V2(zs)]

    here = chord(0)
    here_rolled = [pltpu.roll(t, LANES - 1, 1) for t in here]
    before = None
    for c in range(CH):
        zs = pl.ds(c * LANES, LANES)
        if c < CH - 1:
            after = chord(c + 1)
            after_rolled = [pltpu.roll(t, LANES - 1, 1) for t in after]
        else:
            after = after_rolled = [jnp.zeros((NYB, LANES), F32)] * 5
        f, v2 = here[:4], here[4]
        up = [jnp.where(last_lane, after_rolled[i], here_rolled[i]) for i in range(5)]
        w = v2 + up[4]
        pos = w > 0
        flux = [jnp.where(pos, f[k], up[k]) * w for k in range(4)]
        rolled = [pltpu.roll(t, 1, 1) for t in flux]
        if c == 0:
            edge = jnp.minimum(v2, 0.0)
            before = [edge * f[k] for k in range(4)]
        acc = [f[k] - (flux[k] - jnp.where(first_lane, before[k], rolled[k])) for k in range(4)]
        before = rolled

        v1 = V1(zs)
        w = v1 + jnp.where(last_row, VN(1, zs), pltpu.roll(v1, NYB - 1, 0))
        pos = w > 0
        w_low = VN(0, zs) + v1[0:1]
        pos_low = w_low > 0
        for k in range(4):
            upper = jnp.where(last_row, NR(1, k, zs), pltpu.roll(f[k], NYB - 1, 0))
            flux_k = jnp.where(pos, f[k], upper) * w
            low = jnp.where(pos_low, NR(0, k, zs), f[k][0:1]) * w_low
            acc[k] = acc[k] - (flux_k - jnp.where(first_row, low, pltpu.roll(flux_k, 1, 0)))

        v0 = V0(0, zs)
        w = v0 + V0(1, zs)
        w_low = V0(-1, zs) + v0
        pos, pos_low = w > 0, w_low > 0
        for k in range(4):
            flux_k = jnp.where(pos, f[k], S(k, 1, zs)) * w
            low = jnp.where(pos_low, S(k, -1, zs), f[k]) * w_low
            acc[k] = acc[k] - (flux_k - low)

        pull = pseudo_step * DRAG(zs)
        for k in range(3):
            acc[1 + k] = acc[1 + k] + pull * (f[0] * AIR(k, zs) - f[1 + k])
        emit(c, zs, acc, v0, v1, v2)
        here, here_rolled = after, after_rolled


def advance(S, V0, V1, V2, VN, NR, AIR, DRAG, emit, x):
    sweep_layer(
        lambda k, d, zs: S[k, x + d, :, zs],
        lambda d, zs: V0[x + d, :, zs],
        lambda zs: V1[x - 1, :, zs],
        lambda zs: V2[x - 1, :, zs],
        lambda side, zs: VN[side, x - 1, :, zs],
        lambda side, k, zs: NR[side, k, x - 1, :, zs],
        lambda k, zs: AIR[k, x - 1, :, zs],
        lambda zs: DRAG[x - 1, :, zs],
        emit,
    )


def prepare(owner_ref, face_ref, rank_ref, key8_ref, send_ref, hot_ref, n, h):
    q_len = 256
    quarters = NZ // q_len
    tri = (iota((q_len, q_len), 0) <= iota((q_len, q_len), 1)).astype(F32).astype(BF16)
    names = iota((OWNERS, q_len), 0)
    mine = N_NORMAL * iota((N_SPAN, NZ), 0) + n
    slot = iota((SLOTS, NZ), 0)
    pieces = []
    for b in range(4):
        offset = jnp.zeros((OWNERS, 1), F32)
        got = jnp.zeros((N_SPAN, 2 * SLOTS), F32)
        for half in range(2):
            x = h * 8 + b * 2 + half
            owner = owner_ref[x]
            hots = []
            for q in range(quarters):
                qs = slice(q * q_len, (q + 1) * q_len)
                hot = (owner[:, qs] == names).astype(F32).astype(BF16)
                hot_ref[x, :, qs] = hot
                hots.append(hot)
            counts = jnp.dot(
                jnp.concatenate(hots, axis=0), tri, preferred_element_type=F32
            )
            ranks = []
            for q in range(quarters):
                part = counts[q * OWNERS : (q + 1) * OWNERS]
                ranks.append(
                    jnp.sum(hots[q].astype(F32) * (part + offset), axis=0, keepdims=True) - 1.0
                )
                offset = offset + part[:, q_len - 1 : q_len]
            rank = jnp.concatenate(ranks, axis=1).astype(I32)
            rank_ref[x] = rank
            key = owner * SLOTS + rank
            for t in range(CH):
                key8_ref[x, t : t + 1, :] = key[:, t * LANES : (t + 1) * LANES]
            face = face_ref[x : x + 1, :]
            at = slot == rank
            high = jnp.where(at, (face >> 7).astype(F32), 0.0)
            low = jnp.where(at, (face & 127).astype(F32), 0.0)
            placed = jnp.concatenate([high, low], axis=0).astype(BF16)
            hot16 = (owner == mine).astype(F32).astype(BF16)
            got = got + lax.dot_general(hot16, placed, NT, preferred_element_type=F32)
        pieces.append(got[:, :SLOTS] * 128.0 + got[:, SLOTS:])
    send_ref[:, h, :] = jnp.concatenate(pieces, axis=1).astype(I32)


PR = 24
FR = (0, 1, 2)
MS = (3, 4)
MN = (5, 6, 7)
MC = (8, 9)
AN = (10, 11)
DR = (12, 13)
NEAR = (0, 1, 3, 4, 5, 6, 8, 10, 12)
FAR = (0, 3, 5)
STRIP = len(NEAR) + len(FAR)


def flux_of(w, low, high):
    return jnp.where(w > 0, low, high) * w


def wall_strip(pk, vq, q1, wv):
    lane = iota((PR, LANES), 1)
    last_lane, first_lane = lane == LANES - 1, lane == 0

    def tile(ref, i, t):
        return ref[i, :, t * LANES : (t + 1) * LANES]

    def next_tile(ref, i, t):
        here = pltpu.roll(tile(ref, i, t), LANES - 1, 1)
        if t == CH - 1:
            return jnp.where(last_lane, 0.0, here)
        return jnp.where(last_lane, pltpu.roll(tile(ref, i, t + 1), LANES - 1, 1), here)

    def spanwise(f, v):
        flux = flux_of(v + pltpu.roll(v, PR - 1, 0), f, pltpu.roll(f, PR - 1, 0))
        return flux - pltpu.roll(flux, 1, 0)

    def chordwise(ref, i, f, v, v_next, t, before):
        flux = flux_of(v + v_next, f, next_tile(ref, i, t))
        rolled = pltpu.roll(flux, 1, 1)
        if t == 0:
            before = jnp.minimum(v, 0.0) * f
        return flux - jnp.where(first_lane, before, rolled), rolled

    for y in range(3):
        for t in range(CH):
            zs = slice(t * LANES, (t + 1) * LANES)
            scale = half_step / tile(pk, FR[y], t)
            vq[2 + y, :, zs] = tile(pk, MN[y], t) * scale
            if y < 2:
                vq[y, :, zs] = tile(pk, MS[y], t) * scale
                vq[5 + y, :, zs] = tile(pk, MC[y], t) * scale

    before = [None] * 3
    for t in range(CH):
        zs = slice(t * LANES, (t + 1) * LANES)
        v0, v0_1 = tile(vq, 0, t), tile(vq, 1, t)
        v1, v1_1, v1_2 = tile(vq, 2, t), tile(vq, 3, t), tile(vq, 4, t)
        v2, v2_1 = tile(vq, 5, t), tile(vq, 6, t)
        v2_next, v2_1_next = next_tile(vq, 5, t), next_tile(vq, 6, t)
        a0, a1 = tile(pk, FR[0], t), tile(pk, FR[1], t)
        m0, m1, m2 = (tile(pk, i, t) for i in MN)
        w0, w1 = v1 + v1_1, v1_1 + v1_2
        wall = jnp.minimum(v1, 0.0)
        along, before[0] = chordwise(pk, FR[0], a0, v2, v2_next, t, before[0])
        q1[0, :, zs] = (
            a0 - along - spanwise(a0, v0) - (flux_of(w0, a0, a1) - wall * a0)
        )
        between = flux_of(w0, m0, m1)
        along, before[1] = chordwise(pk, MN[0], m0, v2, v2_next, t, before[1])
        q1[1, :, zs] = (
            m0 - along - spanwise(m0, v0) - (between - wall * m0)
            + pseudo_step * tile(pk, DR[0], t) * (a0 * tile(pk, AN[0], t) - m0)
        )
        along, before[2] = chordwise(pk, MN[1], m1, v2_1, v2_1_next, t, before[2])
        q1[2, :, zs] = (
            m1 - along - spanwise(m1, v0_1) - (flux_of(w1, m1, m2) - between)
            + pseudo_step * tile(pk, DR[1], t) * (a1 * tile(pk, AN[1], t) - m1)
        )

    before = None
    for t in range(CH):
        zs = slice(t * LANES, (t + 1) * LANES)
        v0, v1, v1_1, v2 = (tile(vq, i, t) for i in (0, 2, 3, 5))
        a0, m0, m1 = (tile(q1, i, t) for i in range(3))
        along, before = chordwise(q1, 1, m0, v2, next_tile(vq, 5, t), t, before)
        out = (
            m0 - along - spanwise(m0, v0)
            - (flux_of(v1 + v1_1, m0, m1) - jnp.minimum(v1, 0.0) * m0)
            + pseudo_step * tile(pk, DR[0], t) * (a0 * tile(pk, AN[0], t) - m0)
        )
        catch = jnp.maximum(-out, 0.0)
        wv[0, :, zs] = catch
        wv[1, :, zs] = (
            catch * (0.5 / (half_step * half_step)) * (v0 * v0 + v1 * v1 + v2 * v2)
        )


def main_kernel(
    a_hbm, m_hbm, air_hbm, drag_hbm, owner_hbm, face_hbm,
    film_hbm, ice_hbm, cool_hbm, shed_hbm, share_hbm, up_hbm,
    frac_out, mom_out, film_out, ice_out, all_ref, key8_ref,
    owner_ref, face_ref, film_ref, ice_ref, cool_ref, shed_ref, share_ref, up_ref,
    s_ref, s1_ref, v0_ref, v1_ref, v2_ref, vn_ref, ns_ref, nr_ref, nr2_ref, air_ref, drag_ref,
    owner_hot, rank_ref, sendface_ref, pk, vq, q1, wv, strip_out, strip_in,
    slots_ref, fw_ref, got_ref, gotface_ref, prevface_ref, lhs_ref, hot_ref, gone_ref,
    links_ref, weight_ref, prev_ref, out_ref, pack_ref, prevpack_ref, back_ref, col_ref,
    load_sem, small_sem, span_send, span_recv, normal_send, normal_recv, strip_send, strip_recv, sends, recvs, ready,
):
    c, n = lax.axis_index("span"), lax.axis_index("normal")
    right, left = (c + 1) % N_SPAN, (c + N_SPAN - 1) % N_SPAN
    on_wall, has_low, has_high = n == 0, n > 0, n < N_NORMAL - 1
    off_wall = has_low
    last_of_column = n == N_NORMAL - 1
    has_next = jnp.logical_or(has_high, c < N_SPAN - 1)
    has_prev = jnp.logical_or(has_low, c > 0)
    next_c, next_n = jnp.where(last_of_column, c + 1, c), jnp.where(last_of_column, 0, n + 1)
    prev_c, prev_n = jnp.where(on_wall, c - 1, c), jnp.where(on_wall, N_NORMAL - 1, n - 1)
    cross_next = jnp.logical_and(last_of_column, c < N_SPAN - 1)
    cross_prev = jnp.logical_and(on_wall, c > 0)

    first_loads = [
        pltpu.make_async_copy(src, dst, small_sem.at[i])
        for i, (src, dst) in enumerate(((owner_hbm, owner_ref), (face_hbm, face_ref)))
    ]
    low, high = pl.ds(0, 8), pl.ds(8, 8)
    whole = pl.ds(1, NX)
    low_loads = [
        pltpu.make_async_copy(src, dst, load_sem.at[i])
        for i, (src, dst) in enumerate(
            (
                (a_hbm.at[:, low], s_ref.at[0, whole, low]),
                (m_hbm.at[:, :, low], s_ref.at[pl.ds(1, 3), whole, low]),
                (air_hbm.at[1, :, low], air_ref.at[1, :, low]),
                (drag_hbm.at[:, low], drag_ref.at[:, low]),
            )
        )
    ]
    loads = [
        pltpu.make_async_copy(src, dst, load_sem.at[4 + i])
        for i, (src, dst) in enumerate(
            (
                (a_hbm.at[:, high], s_ref.at[0, whole, high]),
                (m_hbm.at[:, :, high], s_ref.at[pl.ds(1, 3), whole, high]),
                (air_hbm.at[1, :, high], air_ref.at[1, :, high]),
                (drag_hbm.at[:, high], drag_ref.at[:, high]),
                (air_hbm.at[0], air_ref.at[0]),
                (air_hbm.at[2], air_ref.at[2]),
            )
        )
    ] + [
        pltpu.make_async_copy(src, dst, small_sem.at[2 + i])
        for i, (src, dst) in enumerate(
            ((film_hbm, film_ref), (ice_hbm, ice_ref), (cool_hbm, cool_ref), (shed_hbm, shed_ref),
             (share_hbm, share_ref), (up_hbm, up_ref))
        )
    ]
    for load in first_loads + low_loads + loads:
        load.start()

    barrier = pltpu.get_barrier_semaphore()

    @pl.loop(1, N_SPAN)
    def _(i):
        pl.semaphore_signal(barrier, 1, device_id=((c + i) % N_SPAN, n), device_id_type=MESH)

    @pl.loop(1, N_NORMAL)
    def _(i):
        pl.semaphore_signal(barrier, 1, device_id=(c, (n + i) % N_NORMAL), device_id_type=MESH)

    @pl.when(cross_next)
    def _():
        pl.semaphore_signal(barrier, 1, device_id=(next_c, next_n), device_id_type=MESH)

    @pl.when(cross_prev)
    def _():
        pl.semaphore_signal(barrier, 1, device_id=(prev_c, prev_n), device_id_type=MESH)

    for load in first_loads:
        load.wait()
    prepare(owner_ref, face_ref, rank_ref, key8_ref, sendface_ref, owner_hot, n, 0)
    for load in low_loads:
        load.wait()

    def packed_row(i, x):
        if i in FR:
            return s_ref[0, x + 1, FR.index(i) : FR.index(i) + 1, :]
        for k, sets in ((1, MS), (2, MN), (3, MC)):
            if i in sets:
                y = sets.index(i)
                return s_ref[k, x + 1, y : y + 1, :]
        if i in AN:
            return air_ref[1, x, AN.index(i) : AN.index(i) + 1, :]
        return drag_ref[x, DR.index(i) : DR.index(i) + 1, :]

    @pl.when(on_wall)
    def _():
        for side, near, far in ((0, NX - 1, NX - 2), (1, 0, 1)):
            for j, i in enumerate(NEAR):
                strip_out[side, j] = packed_row(i, near)
            for j, i in enumerate(FAR):
                strip_out[side, len(NEAR) + j] = packed_row(i, far)

    @pl.when(jnp.logical_not(has_prev))
    def _():
        prev_ref[...] = jnp.zeros((8, LANES), F32)
        prevpack_ref[...] = jnp.ones((4, 8, LANES), F32)
        prevface_ref[...] = jnp.zeros((N_SPAN, 2, LANES), I32)

    crossing = jnp.logical_or(cross_next, cross_prev)
    peers = N_SPAN + N_NORMAL - 2

    @pl.when(crossing)
    def _():
        pl.semaphore_wait(barrier, peers + 1)

    @pl.when(jnp.logical_not(crossing))
    def _():
        pl.semaphore_wait(barrier, peers)

    def remote(src, dst, send, recv, device):
        return pltpu.make_async_remote_copy(
            src_ref=src, dst_ref=dst, send_sem=send, recv_sem=recv,
            device_id=device, device_id_type=MESH,
        )

    def await_bytes(ref, sem):
        pltpu.make_async_copy(ref, ref, sem).wait()

    def far_first(place, i):
        return (place + jnp.where(i == 3, 0, jnp.where(i == 0, 2, 2 * i - 1))) & 3

    def row_peer(i):
        return far_first(c >> 2, i >> 2) * 4 + far_first(c & 3, i & 3)

    sides = [2 * ((n >> 1) + j & 3) + core for j in (2, 1, 3, 0) for core in range(2)]
    here_last = [2 * ((n >> 1) + j & 3) + core for j in (2, 1, 3) for core in range(2)] + [n ^ 1]

    def to_all(src, dst, which):
        @pl.loop(0, N_SPAN - 1)
        def _(i):
            there = row_peer(i)
            for side in sides:
                remote(src(there, side), dst, sends.at[which], recvs.at[which],
                       (there, side)).start()

        for side in here_last:
            remote(src(c, side), dst, sends.at[which], recvs.at[which], (c, side)).start()

    def to_row(src, dst, which):
        @pl.loop(0, N_SPAN - 1)
        def _(i):
            there = row_peer(i)
            remote(src.at[there], dst.at[c], sends.at[which], recvs.at[which], (there, n)).start()

    strips = [
        remote(
            strip_out.at[side], strip_in.at[side], strip_send.at[side], strip_recv.at[side],
            (there, n),
        )
        for side, there in ((0, right), (1, left))
    ]

    @pl.when(on_wall)
    def _():
        for copy in strips:
            copy.start()

        @pl.loop(1, N_SPAN)
        def _(i):
            pl.semaphore_signal(ready, 1, device_id=((c + i) % N_SPAN, n), device_id_type=MESH)

    def normal_copies(base, dst, sem, start, size):
        part = pl.ds(start, size)
        return (
            remote(ns_ref.at[base, 0, :, part], dst.at[1, :, part], normal_send.at[2 * sem],
                   normal_recv.at[2 * sem], (c, n - 1)),
            remote(ns_ref.at[base, 1, :, part], dst.at[0, :, part], normal_send.at[2 * sem + 1],
                   normal_recv.at[2 * sem + 1], (c, n + 1)),
        )

    def start_normal(*which):
        low, high = normal_copies(*which)

        @pl.when(has_low)
        def _():
            low.start()

        @pl.when(has_high)
        def _():
            high.start()

    def wait_normal(*which):
        low, high = normal_copies(*which)

        @pl.when(has_low)
        def _():
            low.wait_send()
            high.wait_recv()

        @pl.when(has_high)
        def _():
            high.wait_send()
            low.wait_recv()

    def close_edges(dst):
        @pl.when(jnp.logical_not(has_low))
        def _():
            dst[0] = jnp.zeros(dst.shape[1:], F32)

        @pl.when(jnp.logical_not(has_high))
        def _():
            dst[1] = jnp.zeros(dst.shape[1:], F32)

    def span_copies(src, dst, base):
        return [
            remote(src.at[:, layer], dst.at[:, target], span_send.at[base + i],
                   span_recv.at[base + i], (there, n))
            for i, (there, layer, target) in enumerate(((right, NX, 0), (left, 1, NX + 1)))
        ]

    for load in loads:
        load.wait()

    @pl.loop(0, NX)
    def _(x):
        for k in range(4):
            ns_ref[0, 0, k, x] = s_ref[k, x + 1, 0:1, :]
            ns_ref[0, 1, k, x] = s_ref[k, x + 1, NYB - 1 : NYB, :]

    parts = ((1, 8), (9, 7), (0, 1))
    first_halo = [(0, nr_ref, i, start, size) for i, (start, size) in enumerate(parts)]
    again_halo = [(1, nr2_ref, 3 + i, start, size) for i, (start, size) in enumerate(parts)]
    for halo in first_halo:
        start_normal(*halo)
    close_edges(nr_ref)
    close_edges(nr2_ref)
    spans = span_copies(s_ref, s_ref, 0)
    for copy in spans:
        copy.start()
    film0 = film_ref[...]
    shed = shed_ref[...]
    outflow0 = film0 * shed
    out_ref[...] = outflow0

    def pass_on(src, dst, which):
        return remote(src, dst, sends.at[which], recvs.at[which], (next_c, next_n))

    @pl.when(has_next)
    def _():
        pass_on(out_ref, prev_ref, 1).start()

    prepare(owner_ref, face_ref, rank_ref, key8_ref, sendface_ref, owner_hot, n, 1)
    to_row(sendface_ref, gotface_ref, 0)
    gotface_ref[c] = sendface_ref[c]

    @pl.loop(0, NX)
    def _(x):
        scale = half_step / s_ref[0, x + 1]
        v0_ref[x + 1] = s_ref[1, x + 1] * scale
        v1_ref[x] = s_ref[2, x + 1] * scale
        v2_ref[x] = s_ref[3, x + 1] * scale

    @pl.when(on_wall)
    def _():
        for i in range(14):
            pk[i, 0:8, :] = jnp.ones((8, NZ), F32)
            pk[i, 16:24, :] = jnp.ones((8, NZ), F32)
        for x in range(NX):
            for i in range(14):
                pk[i, x + 2 : x + 3, :] = packed_row(i, x)
        for copy in strips:
            copy.wait()
        for side, near, far in ((0, 1, 0), (1, NX + 2, NX + 3)):
            for j, i in enumerate(NEAR):
                pk[i, near : near + 1, :] = strip_in[side, j]
            for j, i in enumerate(FAR):
                pk[i, far : far + 1, :] = strip_in[side, len(NEAR) + j]
        wall_strip(pk, vq, q1, wv)
        slot = iota((SLOTS, NZ), 0)

        @pl.loop(0, NX // 2, unroll=2)
        def _(b):
            total = jnp.zeros((4 * SLOTS, OWNERS), F32)
            for half in range(2):
                x = b * 2 + half
                at = slot == rank_ref[x]
                rows = []
                for split in range(2):
                    for v in range(2):
                        value = wv[v, pl.ds(x + 2, 1), :]
                        high = value.astype(BF16).astype(F32)
                        rows.append(jnp.where(at, high if split == 0 else value - high, 0.0))
                weights = jnp.concatenate(rows, axis=0).astype(BF16)
                total = total + lax.dot_general(
                    weights, owner_hot[x], NT, preferred_element_type=F32
                )
            both = total[: 2 * SLOTS] + total[2 * SLOTS :]
            spot = pl.ds(pl.multiple_of(b * SLOTS, SLOTS), SLOTS)
            slots_ref[0, spot, :] = both[:SLOTS]
            slots_ref[1, spot, :] = both[SLOTS:]

        fw_ref[0] = jnp.zeros((4, LANES), F32)
        for v in range(2):
            for h in range(2):
                fw_ref[1:, 2 * v + h, :] = slots_ref[v, h * LANES : (h + 1) * LANES, :].T
        pl.semaphore_wait(ready, N_SPAN - 1)

        to_all(
            lambda there, side: fw_ref.at[pl.ds(there * N_NORMAL + side, 2)], got_ref.at[c], 3
        )
        got_ref[c] = fw_ref[pl.ds(c * N_NORMAL, 2)]

    for k in range(4):
        for t in range(8):
            links_ref[k, t : t + 1, :] = up_ref[k : k + 1, t * LANES : (t + 1) * LANES]
            weight_ref[k, t : t + 1, :] = share_ref[k : k + 1, t * LANES : (t + 1) * LANES]
    lanes_high = iota((LANES, LANES), 0)
    first_face = (c * N_NORMAL + n) * 1024

    def face_tables(faces_ref, which):
        for s in range(2 * N_SPAN):
            face = faces_ref[s // 2][s % 2 : s % 2 + 1]
            hot_ref[which, :, s * LANES : (s + 1) * LANES] = (
                (lanes_high == (face & 127)).astype(F32).astype(BF16)
            )
            back_ref[which, s : s + 1, :] = face

    def runin(before, own):
        total = jnp.zeros((8, LANES), F32)
        for k in range(4):
            link = links_ref[k]
            spot = link - (first_face - 1024)
            low, high = spot & 127, spot >> 7
            picked = jnp.zeros((8, LANES), F32)
            for j in range(16):
                line = before[j : j + 1] if j < 8 else own[j - 8 : j - 7]
                value = jnp.take_along_axis(
                    jnp.broadcast_to(line, (8, LANES)), low, axis=1, mode="promise_in_bounds"
                )
                picked = jnp.where(high == j, value, picked)
            total = total + weight_ref[k] * jnp.where(link >= 0, picked, 0.0)
        return total

    def link_up():
        await_bytes(gotface_ref.at[pl.ds(0, N_SPAN - 1)], recvs.at[0])

        @pl.when(has_next)
        def _():
            pass_on(gotface_ref, prevface_ref, 4).start()

        face_tables(gotface_ref, 1)

        @pl.when(has_prev)
        def _():
            await_bytes(prev_ref, recvs.at[1])

        run0 = runin(prev_ref[...], outflow0)
        for i, value in enumerate((film0, shed, cool_ref[...], run0)):
            pack_ref[i] = value

        @pl.when(has_next)
        def _():
            pass_on(pack_ref, prevpack_ref, 2).start()

    def edge_speed(side, present, start, size):
        @pl.when(present)
        def _():
            @pl.loop(start, start + size)
            def _(x):
                vn_ref[side, x] = nr_ref[side, 2, x] * (half_step / nr_ref[side, 0, x])

    for side, present in ((0, has_low), (1, has_high)):
        @pl.when(jnp.logical_not(present))
        def _():
            vn_ref[side] = jnp.zeros(vn_ref.shape[1:], F32)

    def take_halo(part):
        wait_normal(*first_halo[part])
        for side, present in ((0, has_low), (1, has_high)):
            edge_speed(side, present, *parts[part])

    take_halo(0)
    again = span_copies(s1_ref, s1_ref, 2)

    @pl.loop(0, NX)
    def _(i):
        @pl.when(i == 8)
        def _():
            start_normal(*again_halo[0])
            link_up()
            take_halo(1)
            take_halo(2)
            for copy in spans:
                copy.wait()
            for edge in (0, NX + 1):
                v0_ref[edge] = s_ref[1, edge] * (half_step / s_ref[0, edge])

        @pl.when(i == 10)
        def _():
            for copy in again:
                copy.start()

        x = jnp.where(i < 8, i + 2, jnp.where(i == 8, 1, jnp.where(i == 9, NX, i)))

        def emit(t, zs, acc, v0, v1, v2):
            for k in range(4):
                s1_ref[k, x, :, zs] = acc[k]
                ns_ref[1, 0, k, x - 1, :, zs] = acc[k][0:1]
                ns_ref[1, 1, k, x - 1, :, zs] = acc[k][NYB - 1 : NYB]

        advance(s_ref, v0_ref, v1_ref, v2_ref, vn_ref, nr_ref, air_ref, drag_ref, emit, x)

    start_normal(*again_halo[1])
    start_normal(*again_halo[2])

    @pl.when(has_prev)
    def _():
        await_bytes(prevface_ref, recvs.at[4])
        await_bytes(prevpack_ref, recvs.at[2])

    face_tables(prevface_ref, 0)

    @pl.when(on_wall)
    def _():
        await_bytes(got_ref.at[pl.ds(0, N_SPAN - 1)], recvs.at[3])

    @pl.when(off_wall)
    def _():
        await_bytes(got_ref, recvs.at[3])

    eight = iota((8, LANES), 0)

    def face_sums(which):
        for s in range(2 * N_SPAN):
            at = eight == (back_ref[which, s : s + 1, :] >> 7)
            values = [
                got_ref[s // 2, which, 2 * v + s % 2 : 2 * v + s % 2 + 1, :] for v in range(2)
            ]
            highs = [value.astype(BF16).astype(F32) for value in values]
            rows = []
            for part in (highs, [values[v] - highs[v] for v in range(2)]):
                rows.extend(jnp.where(at, part[v], 0.0) for v in range(2))
            lhs_ref[which, :, s * LANES : (s + 1) * LANES] = (
                jnp.concatenate(rows, axis=0).astype(BF16)
            )
        sums = lax.dot_general(
            lhs_ref[which], hot_ref[which], NT, preferred_element_type=F32
        )
        sums = sums[:16] + sums[16:]
        return sums[:8], sums[8:]

    def film_step(film, outflow, run, catch, heat):
        inflow = impact_rate * catch + film - outflow + run
        frozen = heat * inflow / (heat + inflow)
        return inflow - frozen, frozen

    prev_catch, prev_kinetic = face_sums(0)
    face_catch, face_kinetic = face_sums(1)
    run0 = pack_ref[3]
    heat = cool_ref[...] / (1.0 + face_kinetic)
    prev_film, prev_shed, prev_cool, prev_run = (prevpack_ref[i] for i in range(4))
    prev_film1, _ = film_step(
        prev_film, prev_ref[...], prev_run, prev_catch, prev_cool / (1.0 + prev_kinetic)
    )
    film1, frozen1 = film_step(film0, outflow0, run0, face_catch, heat)
    outflow1 = film1 * shed
    run1 = runin(prev_film1 * prev_shed, outflow1)
    film2, frozen2 = film_step(film1, outflow1, run1, face_catch, heat)
    film_out[...] = film2
    ice2 = ice_ref[...] + frozen1 + frozen2
    ice_out[...] = ice2

    for g in range(4):
        faces = back_ref[1, g * 8 : g * 8 + 8, :]
        low, high = faces & 127, faces >> 7
        picked = jnp.zeros((8, LANES), F32)
        for j in range(8):
            value = jnp.take_along_axis(
                jnp.broadcast_to(ice2[j : j + 1], (8, LANES)), low, axis=1,
                mode="promise_in_bounds",
            )
            picked = jnp.where(high == j, value, picked)
        for i in range(4):
            col_ref[g * 4 + i] = picked[2 * i : 2 * i + 2]
    to_all(lambda there, side: col_ref.at[there], all_ref.at[c * N_NORMAL + n], 5)
    all_ref[c * N_NORMAL + n] = col_ref[c]


    @pl.loop(0, NX)
    def _(i):
        for at, part in ((0, 0), (8, 1), (NX - 2, 2)):
            @pl.when(i == at)
            def _():
                wait_normal(*again_halo[part])

        @pl.when(i == NX - 2)
        def _():
            for copy in again:
                copy.wait()

        x = jnp.where(i < NX - 2, i + 2, jnp.where(i == NX - 2, 1, NX))

        def emit(t, zs, acc, v0, v1, v2):
            frac_out[x - 1, :, zs] = acc[0]
            for k in range(3):
                mom_out[k, x - 1, :, zs] = acc[1 + k]

        advance(s1_ref, v0_ref, v1_ref, v2_ref, vn_ref, nr2_ref, air_ref, drag_ref, emit, x)

    await_bytes(all_ref.at[pl.ds(0, OWNERS - 1)], recvs.at[5])

    await_bytes(sendface_ref.at[pl.ds(0, N_SPAN - 1)], sends.at[0])

    @pl.when(has_next)
    def _():
        await_bytes(out_ref, sends.at[1])
        await_bytes(pack_ref, sends.at[2])
        await_bytes(gotface_ref, sends.at[4])

    @pl.when(on_wall)
    def _():
        await_bytes(gone_ref, sends.at[3])

    await_bytes(all_ref.at[pl.ds(0, OWNERS - 1)], sends.at[5])


def output_kernel(
    frac_ref, mom_ref, film_ref, ice_ref, all_ref, key8_ref,
    frac_out, mom_out, film_out, ice_out, disp_out,
    pick_ref, row_ref, disp_ref, sems,
):
    n = lax.axis_index("normal")
    put_m = pltpu.make_async_copy(mom_ref, mom_out, sems.at[0])
    put_a = pltpu.make_async_copy(frac_ref, frac_out, sems.at[1])
    put_m.start()
    put_a.start()
    put_film = pltpu.make_async_copy(film_ref, film_out, sems.at[6])
    put_ice = pltpu.make_async_copy(ice_ref, ice_out, sems.at[7])
    put_film.start()
    put_ice.start()

    for h in range(2):
        pick_ref[h * LANES : (h + 1) * LANES, :] = (
            all_ref[:, h, :].T
        )
    y = (n * NYB + iota((NYB, LANES), 0)).astype(F32) + 0.5
    left = 1.0 - y / (NYB * N_NORMAL)
    profile = left * left
    group = 4
    puts = []
    for g in range(NX // group):

        @pl.loop(g * group, (g + 1) * group)
        def _(x):
            key = key8_ref[x]
            owner, rank = key >> 5, key & (SLOTS - 1)
            base = pl.multiple_of((x // 2) * SLOTS, SLOTS)
            table = pick_ref[pl.ds(base, SLOTS), :]
            picked = jnp.zeros((8, LANES), F32)
            for j in range(SLOTS):
                value = jnp.take_along_axis(
                    jnp.broadcast_to(table[j : j + 1], (8, LANES)), owner, axis=1,
                    mode="promise_in_bounds",
                )
                picked = jnp.where(rank == j, value, picked)
            row_ref[...] = picked
            for t in range(CH):
                disp_ref[x, :, t * LANES : (t + 1) * LANES] = row_ref[t : t + 1, :] * profile

        part = pl.ds(g * group, group)
        put = pltpu.make_async_copy(disp_ref.at[part], disp_out.at[part], sems.at[2 + g])
        put.start()
        puts.append(put)
    for put in (put_m, put_a, put_film, put_ice):
        put.wait()
    for put in puts:
        put.wait()


def shape(dims, dtype=F32):
    return jax.ShapeDtypeStruct(dims, dtype)


VM = pl.BlockSpec(memory_space=pltpu.VMEM)
HBM = pl.BlockSpec(memory_space=pltpu.HBM)


def per_device(
    volume_fraction, droplet_momentum, air_velocity, drag, wall_owner, wall_face,
    film, ice, cooling, shed, share, upstream,
):
    brick = (NX, NYB, NZ)
    tile = (8, LANES)
    rows = (NX, 1, NZ)
    hbm = functools.partial(pltpu.with_memory_space_constraint, memory_space=pltpu.HBM)
    dma = pltpu.SemaphoreType.DMA
    frac, mom, film_now, ice_now, ice_slots, keys = pl.pallas_call(
        main_kernel,
        out_shape=(
            shape(brick), shape((3,) + brick), shape(tile), shape(tile),
            shape((OWNERS, 2, LANES)), shape((NX, 8, LANES), I32),
        ),
        in_specs=[HBM] * 12,
        out_specs=(VM,) * 6,
        scratch_shapes=[
            pltpu.VMEM(rows, I32),
            pltpu.VMEM((NX, NZ), I32),
            pltpu.VMEM(tile, F32),
            pltpu.VMEM(tile, F32),
            pltpu.VMEM(tile, F32),
            pltpu.VMEM(tile, F32),
            pltpu.VMEM((4, NZ), F32),
            pltpu.VMEM((4, NZ), I32),
            pltpu.VMEM((4, NX + 2, NYB, NZ), F32),
            pltpu.VMEM((4, NX + 2, NYB, NZ), F32),
            pltpu.VMEM((NX + 2, NYB, NZ), F32),
            pltpu.VMEM(brick, F32),
            pltpu.VMEM(brick, F32),
            pltpu.VMEM((2,) + rows, F32),
            pltpu.VMEM((2, 2, 4) + rows, F32),
            pltpu.VMEM((2, 4) + rows, F32),
            pltpu.VMEM((2, 4) + rows, F32),
            pltpu.VMEM((3,) + brick, F32),
            pltpu.VMEM(brick, F32),
            pltpu.VMEM((NX, OWNERS, NZ), BF16),
            pltpu.VMEM(rows, I32),
            pltpu.VMEM((N_SPAN, 2, LANES), I32),
            pltpu.VMEM((14, PR, NZ), F32),
            pltpu.VMEM((7, PR, NZ), F32),
            pltpu.VMEM((3, PR, NZ), F32),
            pltpu.VMEM((2, PR, NZ), F32),
            pltpu.VMEM((2, STRIP, 1, NZ), F32),
            pltpu.VMEM((2, STRIP, 1, NZ), F32),
            pltpu.VMEM((2, 8 * SLOTS, OWNERS), F32),
            pltpu.VMEM((OWNERS + 1, 4, LANES), F32),
            pltpu.VMEM((N_SPAN, 2, 4, LANES), F32),
            pltpu.VMEM((N_SPAN, 2, LANES), I32),
            pltpu.VMEM((N_SPAN, 2, LANES), I32),
            pltpu.VMEM((2, 32, 2 * N_SPAN * LANES), BF16),
            pltpu.VMEM((2, LANES, 2 * N_SPAN * LANES), BF16),
            pltpu.VMEM((OWNERS - 1, 8, LANES), F32),
            pltpu.VMEM((4, 8, LANES), I32),
            pltpu.VMEM((4, 8, LANES), F32),
            pltpu.VMEM((8, LANES), F32),
            pltpu.VMEM((8, LANES), F32),
            pltpu.VMEM((4, 8, LANES), F32),
            pltpu.VMEM((4, 8, LANES), F32),
            pltpu.VMEM((2, 2 * N_SPAN, LANES), I32),
            pltpu.VMEM((N_SPAN, 2, LANES), F32),
            dma((10,)), dma((8,)), dma((4,)), dma((4,)), dma((12,)), dma((12,)), dma((2,)), dma((2,)),
            dma((6,)), dma((6,)), pltpu.SemaphoreType.REGULAR,
        ],
        compiler_params=pltpu.CompilerParams(
            collective_id=0, has_side_effects=True, vmem_limit_bytes=40 * MB
        ),
        name="accretion",
    )(
        *map(
            hbm,
            (
                volume_fraction, droplet_momentum, air_velocity, drag,
                wall_owner.reshape(rows), wall_face,
                film.reshape(tile), ice.reshape(tile), cooling.reshape(tile), shed.reshape(tile),
                share, upstream,
            ),
        )
    )

    fraction_out, momentum_out, film_out, ice_out, displacement = pl.pallas_call(
        output_kernel,
        out_shape=(
            shape(brick), shape((3,) + brick), shape(tile), shape(tile), shape(brick),
        ),
        in_specs=[VM] * 6,
        out_specs=(HBM,) * 5,
        scratch_shapes=[
            pltpu.VMEM((8 * SLOTS, OWNERS), F32),
            pltpu.VMEM((8, LANES), F32),
            pltpu.VMEM(brick, F32),
            dma((8,)),
        ],
        compiler_params=pltpu.CompilerParams(vmem_limit_bytes=32 * MB),
        name="results",
    )(frac, mom, film_now, ice_now, ice_slots, keys)
    return fraction_out, momentum_out, film_out.reshape(-1), ice_out.reshape(-1), displacement


def solution(mesh):
    volume = P("span", "normal", None)
    vector = P(None, "span", "normal", None)
    faces = P(("span", "normal"))
    links = P(None, ("span", "normal"))
    return jax.shard_map(
        per_device,
        mesh=mesh,
        in_specs=(
            volume, vector, vector, volume, P("span", None, None), P("span", None),
            faces, faces, faces, faces, links, links,
        ),
        out_specs=(volume, vector, faces, faces, volume),
        check_vma=False,
    )
```
